32 devices in a mesh: grp: 2 (over y), seq: 16 (over z, x, core).
Axes of the slice: x: 2, y: 2, z: 4, core: 2. Of those that a mesh axis runs over, the one named last changes fastest.
Arguments:
- queries: bfloat16 [4096, 2048], P(('grp', 'seq')), parts along dimension 0, may hold values from -6 to 6
- keys: bfloat16 [4096, 2048], P(('grp', 'seq')), parts along dimension 0, may hold values from -6 to 6
- values: bfloat16 [4096, 2048], P(('grp', 'seq')), parts along dimension 0, may hold values from -6 to 6
- out_grad: bfloat16 [4096, 2048], P(('grp', 'seq')), parts along dimension 0, may hold values from -6 to 6
- filter_taps: float32 [256, 2048], P('seq'), may hold values from -0.375 to 0.375
Outputs:
- q_grad: bfloat16 [4096, 2048], P(('grp', 'seq')), parts along dimension 0
- k_grad: bfloat16 [4096, 2048], P(('grp', 'seq')), parts along dimension 0
- v_grad: bfloat16 [4096, 2048], P(('grp', 'seq')), parts along dimension 0
- filter_grad: float32 [512, 2048], P(('grp', 'seq')), parts along dimension 0
The draws below stay inside these ranges and needn't reach their ends.
There are 2 independent parts, one for each index of `grp`. The reference program is written for one: setup_inputs(seed, part) draws one part's arguments, and reference() takes and returns one part's arrays. A program takes and returns all parts, laid end to end along the dimension named above; an argument that names none is the same for every part. Nothing has to cross between parts.
All inputs are finite; a program needn't handle non-finite values.
Results may differ from the reference program's by a relative error of at most 0.005.
Values may be sent and summed in bfloat16 or wider, within the bound.
No kernel may reach another device: no remote copies, remote signals or barrier semaphores. Data moves between devices by JAX's collectives and lax.ppermute only.
A program may use at most 64 MiB of HBM per device.

```python
import math
import jax
import jax.numpy as jnp

C = 2048
TAPS = 256
SEQLEN = 2048


def spiked(entries, stream_key, source, target, shards_of, factor):
    def block_of(dim):
        return (jnp.arange(entries.shape[dim]) // (entries.shape[dim] // shards_of)).reshape((-1,) + (1,) * (entries.ndim - 1 - dim))

    first = jax.random.permutation(stream_key, shards_of)[block_of(target)]
    second = (block_of(target) + shards_of // 2) % shards_of
    return jnp.where((block_of(source) == first) | (block_of(source) == second), factor * entries, entries)


def shard_levels(key, dims, pieces, smallest, largest):
    factor_of, own = 1.0, jax.random.fold_in(key, 6)
    for position, shards_of in pieces:
        heights = jnp.exp(jax.random.uniform(jax.random.fold_in(own, position), (shards_of,), jnp.float32, smallest / len(pieces), largest / len(pieces)))
        factor_of = factor_of * jnp.repeat(heights, dims[position] // shards_of).reshape([-1 if axis == position else 1 for axis in range(len(dims))])
    return factor_of


def gaussian(own_key, dims, width, reach, cuts=(), dtype=jnp.bfloat16):
    drawn = width * jax.random.normal(own_key, dims, jnp.float32)
    if cuts:
        drawn = drawn * shard_levels(own_key, dims, cuts, -0.22, 0.18)
    return jnp.clip(drawn, -reach, reach).astype(dtype)


def noise_with(own_key, extent, deviation, reach, pieces, heavy, dtype=jnp.bfloat16):
    result = deviation * jax.random.normal(own_key, extent, jnp.float32)
    if pieces:
        result = result * shard_levels(own_key, extent, pieces, -0.22, 0.18)
    return jnp.clip(spiked(result, jax.random.fold_in(own_key, 3), *heavy), -reach, reach).astype(dtype)


def setup_inputs(seed: int = 0, part: int = 0) -> dict:
    streams_of = jax.random.split(jax.random.key(seed), 6)
    own_keys = jax.random.split(jax.random.fold_in(streams_of[5], part), 6)
    return {
        "queries": gaussian(own_keys[0], (SEQLEN, C), 1.0, 6.0, ((0, 16),)),
        "keys": gaussian(own_keys[1], (SEQLEN, C), 1.0, 6.0, ((0, 16),)),
        "values": gaussian(own_keys[2], (SEQLEN, C), 1.0, 6.0, ((0, 16),)),
        "out_grad": noise_with(own_keys[3], (SEQLEN, C), 1.0, 6.0, ((0, 16),), (0, 1, 16, 2.0)),
        "filter_taps": gaussian(streams_of[4], (TAPS, C), TAPS ** -0.5, 0.375, ((0, 16),), jnp.float32),
    }


def reference(queries, keys, values, out_grad, filter_taps):
    product = (keys.astype(jnp.float32) * values.astype(jnp.float32)).astype(jnp.bfloat16)
    gated_grad = (out_grad.astype(jnp.float32) * queries.astype(jnp.float32)).astype(jnp.bfloat16)
    length = queries.shape[0]
    nfft = 2 * length
    zspec = jnp.fft.rfft(product.astype(jnp.float32), n=nfft, axis=0)
    gspec = jnp.fft.rfft(gated_grad.astype(jnp.float32), n=nfft, axis=0)
    hspec = jnp.fft.rfft(filter_taps, n=nfft, axis=0)
    mixed = jnp.fft.irfft(zspec * hspec, n=nfft, axis=0)[:length]
    corr = jnp.fft.irfft(jnp.conj(hspec) * gspec, n=nfft, axis=0)[:length]
    lagged = jnp.fft.irfft(gspec * jnp.conj(zspec), n=nfft, axis=0)[:TAPS]
    q_grad = (out_grad.astype(jnp.float32) * mixed).astype(jnp.bfloat16)
    k_grad = (corr * values.astype(jnp.float32)).astype(jnp.bfloat16)
    v_grad = (corr * keys.astype(jnp.float32)).astype(jnp.bfloat16)
    filter_grad = lagged * (1.0 / math.sqrt(length))
    return (q_grad, k_grad, v_grad, filter_grad)
```

```python
import math

import jax
import jax.numpy as jnp
import numpy as np
from jax import lax
from jax.experimental import pallas as pl
from jax.experimental.pallas import tpu as pltpu
from jax.sharding import PartitionSpec as P

PLANE = 4
CHUNKS = 2
VMEM_BYTES = 48 * 1024 * 1024


def tables(block):
    half = np.concatenate([np.arange(0, block, 2), np.arange(1, block, 2)])
    angle = np.pi * (half[:, None] + 0.5) * np.arange(block)[None, :] / block
    forward = np.concatenate([np.cos(angle), -np.sin(angle)], 0)
    inverse = forward.T / block
    return forward, inverse


def pair(table):
    high = table.astype(np.float32).astype(jnp.bfloat16)
    low = (table - high.astype(np.float64)).astype(np.float32).astype(jnp.bfloat16)
    return jnp.asarray(high), jnp.asarray(low)


def dot(left, right):
    return jnp.dot(left, right, preferred_element_type=jnp.float32)


def spectrum(high, low, block):
    return dot(high[...], block) + dot(low[...], block)


def restore(high, low, real, imag):
    spec = jnp.concatenate([real, imag], 0)
    top = spec.astype(jnp.bfloat16)
    rest = (spec - top.astype(jnp.float32)).astype(jnp.bfloat16)
    return dot(high[...], top) + dot(low[...], top) + dot(high[...], rest)


def parts(spec):
    half = spec.shape[0] // 2
    return spec[:half], spec[half:]


def turned(spec, sign):
    real, imag = parts(spec)
    quarter = real.shape[0] // 2
    flip = lambda a, s: jnp.concatenate([s * a[:quarter], -s * a[quarter:]], 0)
    return flip(imag, -sign), flip(real, sign)


def window(near, far, sign):
    real, imag = parts(near)
    other_real, other_imag = turned(far, sign)
    return real + other_real, imag + other_imag


def times(left, right):
    return left[0] * right[0] - left[1] * right[1], left[0] * right[1] + left[1] * right[0]


def times_conj(left, right):
    return left[0] * right[0] + left[1] * right[1], left[1] * right[0] - left[0] * right[1]


def call(body, outs, args, scratch=(), flops=0):
    specs = [
        pl.BlockSpec(memory_space=pltpu.SMEM if a.ndim == 1 else pltpu.VMEM) for a in args
    ]
    nbytes = sum(math.prod(a.shape) * a.dtype.itemsize for a in list(args) + list(outs))
    return pl.pallas_call(
        body,
        out_shape=outs,
        in_specs=specs,
        out_specs=[pl.BlockSpec(memory_space=pltpu.VMEM)] * len(outs),
        scratch_shapes=scratch,
        compiler_params=pltpu.CompilerParams(vmem_limit_bytes=VMEM_BYTES),
        cost_estimate=pl.CostEstimate(flops=flops, bytes_accessed=nbytes, transcendentals=0),
    )(*args)


def shards(queries, keys, values, out_grad, filter_taps):
    f32, bf16 = jnp.float32, jnp.bfloat16
    rows, channels = queries.shape
    nseq = lax.axis_size("seq")
    own_taps = filter_taps.shape[0]
    taps = own_taps * nseq
    planes = nseq // PLANE
    width = channels // PLANE
    part = width // CHUNKS
    tokens = rows * PLANE
    pad_taps = max(16, own_taps)
    plane_taps = taps // planes
    filter_rows = CHUNKS * pad_taps
    assert tokens == 2 * taps
    me = lax.axis_index("seq")
    place = jnp.stack([me % PLANE, me // PLANE]).astype(jnp.int32)
    devices = range(nseq)

    forward, inverse = tables(taps)
    fwd = pair(forward)
    inv = pair(inverse)
    lag_of = np.full((planes * PLANE, pad_taps), -1)
    lag_of[:, :own_taps] = np.arange(taps).reshape(planes * PLANE, own_taps)
    lag_of = lag_of.reshape(-1)
    fwd_lag = pair(np.where(lag_of[None, :] >= 0, forward[:, np.maximum(lag_of, 0)], 0.0))

    def swap(array, distance):
        return lax.ppermute(array, "seq", [(i, i ^ distance) for i in devices])

    def struct(r, c, dtype):
        return jax.ShapeDtypeStruct((r, c), dtype)

    def gate(place_ref, q_ref, k_ref, v_ref, o_ref, taps_ref, *outs):
        q = place_ref[0]
        for chunk in range(CHUNKS):
            for step in range(PLANE):
                out = outs[chunk * PLANE + step]
                start = pl.multiple_of((q ^ step) * width + chunk * part, part)
                lanes = pl.ds(start, part)
                out[:rows] = (k_ref[:, lanes].astype(f32) * v_ref[:, lanes].astype(f32)).astype(bf16)
                out[rows : 2 * rows] = (
                    o_ref[:, lanes].astype(f32) * q_ref[:, lanes].astype(f32)
                ).astype(bf16)
                if chunk == 0:
                    for piece in range(CHUNKS):
                        start = pl.multiple_of((q ^ step) * width + piece * part, part)
                        block = taps_ref[:, pl.ds(start, part)]
                        if pad_taps > own_taps:
                            block = jnp.concatenate(
                                [block, jnp.zeros((pad_taps - own_taps, part), f32)], 0
                            )
                        first = 2 * rows + piece * pad_taps
                        out[first : first + pad_taps] = block.astype(bf16)

    sent = call(
        gate,
        [
            struct(2 * rows + (filter_rows if chunk == 0 else 0), part, bf16)
            for chunk in range(CHUNKS)
            for _ in range(PLANE)
        ],
        [place, queries, keys, values, out_grad, filter_taps],
    )

    def gather_plane(chunk):
        def body(place_ref, *refs):
            q = place_ref[0]
            ins, outs = refs[:PLANE], refs[PLANE:]
            product, grad, first, second = outs[:4]
            for step in range(PLANE):
                origin = q ^ step
                at = pl.ds(pl.multiple_of(origin * rows, rows), rows)
                product[at] = ins[step][:rows]
                grad[at] = ins[step][rows : 2 * rows]
                if chunk == 0:
                    for piece in range(CHUNKS):
                        begin = 2 * rows + piece * pad_taps
                        to = pl.multiple_of((piece * PLANE + origin) * pad_taps, pad_taps)
                        outs[4][pl.ds(to, pad_taps)] = ins[step][begin : begin + pad_taps]
            even = place_ref[1] % 2 == 0
            last = product[tokens - taps :]
            begin = grad[:taps]
            first[...] = jnp.where(even, last, begin)
            second[...] = jnp.where(even, begin, last)

        mine = sent[chunk * PLANE : (chunk + 1) * PLANE]
        received = [mine[0]] + [swap(mine[step], step) for step in range(1, PLANE)]
        outs = [struct(tokens, part, bf16)] * 2 + [struct(taps, part, bf16)] * 2
        if chunk == 0:
            outs = outs + [struct(PLANE * filter_rows, part, bf16)]
        return call(body, outs, [place] + received)

    lower = [(i, i ^ PLANE) for i in devices]
    upper = [
        (i, (i + PLANE) if (i // PLANE) % 2 == 1 else (i - PLANE))
        for i in devices
        if PLANE <= i < nseq - PLANE
    ]

    def own_spectra(product, grad):
        def body(high, low, p_ref, g_ref, *outs):
            for n, ref in enumerate((p_ref, g_ref)):
                for block in range(2):
                    outs[2 * n + block][...] = spectrum(
                        high, low, ref[block * taps : (block + 1) * taps]
                    )

        return call(
            body,
            [struct(2 * taps, part, f32)] * 4,
            [*fwd, product, grad],
            flops=2 * 2 * 4 * 2 * taps * taps * part,
        )

    def filter_side(spectra, first, second, earlier):
        chunk = len(earlier)
        final = chunk == CHUNKS - 1

        def body(place_ref, high, low, inv_high, inv_low, p0, p1, g0, g1, a_ref, b_ref, *refs):
            before, outs = refs[:chunk], refs[chunk:]
            even = place_ref[1] % 2 == 0
            behind = jnp.where(even, b_ref[...], a_ref[...])
            ahead = jnp.where(even, a_ref[...], b_ref[...])
            spec_behind = spectrum(high, low, behind)
            outs[0][...] = spec_behind
            outs[1][...] = spectrum(high, low, ahead)
            one = times_conj(parts(g0[...]), window(p0[...], spec_behind, 1.0))
            two = times_conj(parts(g1[...]), window(p1[...], p0[...], 1.0))
            lags = restore(inv_high, inv_low, one[0] + two[0], one[1] + two[1])
            if not final:
                outs[2][...] = lags
                return
            full = refs[-1]
            for n in range(chunk):
                full[:, n * part : (n + 1) * part] = before[n][...]
            full[:, chunk * part :] = lags
            z = place_ref[1]
            for step in range(planes):
                at = pl.multiple_of((z ^ step) * plane_taps, plane_taps)
                block = full[pl.ds(at, plane_taps)]
                outs[2 + step][...] = block.astype(outs[2 + step].dtype)

        outs = [struct(2 * taps, part, f32)] * 2
        if final:
            outs = outs + [struct(plane_taps, width, f32)]
            outs = outs + [struct(plane_taps, width, bf16)] * (planes - 1)
        else:
            outs = outs + [struct(taps, part, f32)]
        return call(
            body,
            outs,
            [place, *fwd, *inv, *spectra, first, second, *earlier],
            scratch=[pltpu.VMEM((taps, width), f32)] if final else (),
            flops=2 * (2 * 2 + 3) * 2 * taps * taps * part,
        )

    def signal_side(chunk, spectra, spec_behind, spec_ahead, pieces):
        def body(place_ref, high, low, inv_high, inv_low, p0, p1, g0, g1, pb, ga, *refs):
            ins, outs = refs[:planes], refs[planes : planes + PLANE]
            filt, mixed, corr = refs[planes + PLANE :]
            q, z = place_ref[0], place_ref[1]
            span = PLANE * pad_taps
            for step in range(planes):
                at = pl.multiple_of((z ^ step) * span, span)
                filt[pl.ds(at, span)] = ins[step][chunk * span : (chunk + 1) * span]
            taps_spec = parts(spectrum(high, low, filt[...]))
            behind = (pb, p0, p1)
            ahead = (g0, g1, ga)
            for block in range(2):
                at = slice(block * taps, (block + 1) * taps)
                spec = window(behind[block + 1][...], behind[block][...], 1.0)
                mixed[at] = restore(inv_high, inv_low, *times(taps_spec, spec)).astype(bf16)
                spec = window(ahead[block][...], ahead[block + 1][...], -1.0)
                corr[at] = restore(inv_high, inv_low, *times_conj(spec, taps_spec)).astype(bf16)
            for step in range(PLANE):
                at = pl.ds(pl.multiple_of((q ^ step) * rows, rows), rows)
                outs[step][:rows] = mixed[at]
                outs[step][rows:] = corr[at]

        return call(
            body,
            [struct(2 * rows, part, bf16)] * PLANE,
            [place, *fwd_lag, *inv, *spectra, spec_behind, spec_ahead, *pieces],
            scratch=[
                pltpu.VMEM((planes * PLANE * pad_taps, part), bf16),
                pltpu.VMEM((tokens, part), bf16),
                pltpu.VMEM((tokens, part), bf16),
            ],
            flops=2 * (2 + 4 * 3) * 2 * taps * taps * part,
        )

    def finish(place_ref, k_ref, v_ref, o_ref, *refs):
        ins, (dq, dk, dv) = refs[: CHUNKS * PLANE], refs[CHUNKS * PLANE :]
        q = place_ref[0]
        for chunk in range(CHUNKS):
            for step in range(PLANE):
                block = ins[chunk * PLANE + step]
                start = pl.multiple_of((q ^ step) * width + chunk * part, part)
                lanes = pl.ds(start, part)
                mixed = block[:rows].astype(f32)
                corr = block[rows:].astype(f32)
                dq[:, lanes] = (o_ref[:, lanes].astype(f32) * mixed).astype(bf16)
                dk[:, lanes] = (corr * v_ref[:, lanes].astype(f32)).astype(bf16)
                dv[:, lanes] = (corr * k_ref[:, lanes].astype(f32)).astype(bf16)

    def lay(place_ref, *refs):
        ins, out = refs[:PLANE], refs[PLANE]
        for step in range(PLANE):
            start = pl.multiple_of((place_ref[0] ^ step) * width, width)
            out[:, pl.ds(start, width)] = ins[step][...]

    gathered = [gather_plane(chunk) for chunk in range(CHUNKS)]
    piece = gathered[0][4]
    pieces = [piece] + [swap(piece, PLANE * step) for step in range(1, planes)]
    spectra, lags, halos = [], [], []
    for chunk in range(CHUNKS):
        product, grad, first, second = gathered[chunk][:4]
        first = lax.ppermute(first, "seq", lower)
        second = lax.ppermute(second, "seq", upper)
        spectra.append(own_spectra(product, grad))
        result = filter_side(spectra[chunk], first, second, lags)
        halos.append(result[:2])
        lags.append(result[2])
    own, *away = result[2:]
    total = own
    for step, block in enumerate(away):
        total = total + swap(block, PLANE * (step + 1)).astype(f32)
    total = total * (1.0 / math.sqrt(rows * nseq))
    ends = []
    for step in range(PLANE):
        block = lax.dynamic_slice_in_dim(total, (place[0] ^ step) * own_taps, own_taps, 0)
        ends.append(swap(block, step) if step else block)
    (filter_grad,) = call(lay, [struct(own_taps, channels, f32)], [place, *ends])

    returned = []
    for chunk in range(CHUNKS):
        outs = signal_side(chunk, spectra[chunk], *halos[chunk], pieces)
        returned += [outs[0]] + [swap(outs[step], step) for step in range(1, PLANE)]
    q_grad, k_grad, v_grad = call(
        finish,
        [struct(rows, channels, bf16)] * 3,
        [place, keys, values, out_grad, *returned],
    )
    return (q_grad, k_grad, v_grad, filter_grad)


def solution(mesh):
    placed = (
        P(("grp", "seq"), None),
        P(("grp", "seq"), None),
        P(("grp", "seq"), None),
        P(("grp", "seq"), None),
        P("seq", None),
    )
    return jax.shard_map(
        shards,
        mesh=mesh,
        in_specs=placed,
        out_specs=(
            P(("grp", "seq"), None),
            P(("grp", "seq"), None),
            P(("grp", "seq"), None),
            P(("grp", "seq"), None),
        ),
        check_vma=False,
    )
```

```python
import math

import jax
import jax.numpy as jnp
import numpy as np
from jax import lax
from jax.experimental import pallas as pl
from jax.experimental.pallas import tpu as pltpu
from jax.sharding import PartitionSpec as P

PLANE = 4
VMEM_BYTES = 32 * 1024 * 1024
LONG = 10**10


def tables(block):
    half = np.concatenate([np.arange(0, block, 2), np.arange(1, block, 2)])
    angle = np.pi * (half[:, None] + 0.5) * np.arange(block)[None, :] / block
    forward = np.concatenate([np.cos(angle), -np.sin(angle)], 0)
    inverse = forward.T / block
    return forward, inverse


def pair(table):
    high = table.astype(np.float32).astype(jnp.bfloat16)
    low = (table - high.astype(np.float64)).astype(np.float32).astype(jnp.bfloat16)
    return jnp.asarray(high), jnp.asarray(low)


def dot(left, right):
    return jnp.dot(left, right, preferred_element_type=jnp.float32)


def spectrum(high, low, block):
    return dot(high[...], block) + dot(low[...], block)


def restore(high, low, real, imag):
    spec = jnp.concatenate([real, imag], 0)
    top = spec.astype(jnp.bfloat16)
    rest = (spec - top.astype(jnp.float32)).astype(jnp.bfloat16)
    return dot(high[...], top) + dot(low[...], top) + dot(high[...], rest)


def parts(spec):
    half = spec.shape[0] // 2
    return spec[:half], spec[half:]


def turned(spec, sign):
    real, imag = parts(spec)
    quarter = real.shape[0] // 2
    flip = lambda a, s: jnp.concatenate([s * a[:quarter], -s * a[quarter:]], 0)
    return flip(imag, -sign), flip(real, sign)


def window(near, far, sign):
    real, imag = parts(near)
    other_real, other_imag = turned(far, sign)
    return real + other_real, imag + other_imag


def times(left, right):
    return left[0] * right[0] - left[1] * right[1], left[0] * right[1] + left[1] * right[0]


def times_conj(left, right):
    return left[0] * right[0] + left[1] * right[1], left[1] * right[0] - left[0] * right[1]


def call(body, outs, args, scratch=(), spaces=None, after=(), flops=1):
    specs = [
        pl.BlockSpec(memory_space=pltpu.SMEM if a.ndim == 1 else pltpu.VMEM) for a in args
    ]
    specs += [pl.BlockSpec(memory_space=pl.ANY)] * len(after)

    def run(*refs):
        body(*refs[: len(args)], *refs[len(args) + len(after) :])

    spaces = spaces or [pltpu.VMEM] * len(outs)
    return pl.pallas_call(
        run,
        out_shape=outs,
        in_specs=specs,
        out_specs=[pl.BlockSpec(memory_space=space) for space in spaces],
        scratch_shapes=scratch,
        compiler_params=pltpu.CompilerParams(vmem_limit_bytes=VMEM_BYTES),
        cost_estimate=pl.CostEstimate(flops=flops, bytes_accessed=1, transcendentals=0),
    )(*args, *after)


def shards(queries, keys, values, out_grad, filter_taps):
    f32, bf16 = jnp.float32, jnp.bfloat16
    rows, channels = queries.shape
    nseq = lax.axis_size("seq")
    own_taps = filter_taps.shape[0]
    taps = own_taps * nseq
    planes = nseq // PLANE
    width = channels // PLANE
    tokens = rows * PLANE
    pad_taps = max(16, own_taps)
    plane_taps = taps // planes
    column = planes * pad_taps
    assert tokens == 2 * taps
    me = lax.axis_index("seq")
    place = jnp.stack([me % PLANE, me // PLANE]).astype(jnp.int32)
    devices = range(nseq)

    forward, inverse = tables(taps)
    fwd = pair(forward)
    inv = pair(inverse)
    lag_of = np.full((planes * PLANE, pad_taps), -1)
    lag_of[:, :own_taps] = np.arange(taps).reshape(planes * PLANE, own_taps)
    lag_of = lag_of.reshape(planes, PLANE, pad_taps).transpose(1, 0, 2).reshape(-1)
    fwd_lag = pair(np.where(lag_of[None, :] >= 0, forward[:, np.maximum(lag_of, 0)], 0.0))

    def swap(array, distance):
        return lax.ppermute(array, "seq", [(i, i ^ distance) for i in devices])

    def shift(array, distance):
        return lax.ppermute(
            array, "seq", [(i, i + distance) for i in devices if i + distance in devices]
        )

    def struct(r, c, dtype):
        return jax.ShapeDtypeStruct((r, c), dtype)

    def block_at(index, size):
        return pl.ds(pl.multiple_of(index * size, size), size)

    def lay_taps(place_ref, *refs):
        ins, (keep, side, full) = refs[:planes], refs[planes:]
        q, z = place_ref[0], place_ref[1]
        for step in range(planes):
            full[block_at(z ^ step, pad_taps)] = ins[step][...]
        for step, (out, half) in enumerate(((keep, 0), (side, 0), (keep, 1), (side, 1))):
            out[half * column : (half + 1) * column] = full[:, block_at(q ^ step, width)]

    def narrow_taps(taps_ref, out):
        out[:own_taps] = taps_ref[...].astype(bf16)
        if pad_taps > own_taps:
            out[own_taps:] = jnp.zeros((pad_taps - own_taps, channels), bf16)

    def gate_grad(place_ref, o_ref, q_ref, p_ref, keep, side):
        q = place_ref[0]
        side[:rows] = p_ref[...]
        for step, (out, first) in enumerate(((keep, 0), (side, rows), (keep, rows), (side, 2 * rows))):
            at = block_at(q ^ step, width)
            out[first : first + rows] = (
                o_ref[:, at].astype(f32) * q_ref[:, at].astype(f32)
            ).astype(bf16)

    def join(left, right, after=()):
        def body(left_ref, right_ref, out):
            out[:rows] = left_ref[left.shape[0] - rows :]
            out[rows:] = right_ref[right.shape[0] - rows :]

        return call(body, [struct(2 * rows, width, bf16)], [left, right], after=after)[0]

    def gather_product(place_ref, *refs):
        ins, (product, top) = refs[:PLANE], refs[PLANE:]
        q = place_ref[0]
        for step in range(PLANE):
            product[block_at(q ^ step, rows)] = ins[step][:rows]
        top[...] = product[tokens - taps :]

    def join_taps(keep, near, ship):
        ship[:column] = keep[column:]
        ship[column:] = near[column:]

    def gather_grad(place_ref, keep, near, far, grad, bottom):
        q = place_ref[0]
        grad[block_at(q, rows)] = keep[:rows]
        grad[block_at(q ^ 1, rows)] = near[rows : 2 * rows]
        grad[block_at(q ^ 2, rows)] = far[:rows]
        grad[block_at(q ^ 3, rows)] = far[rows:]
        bottom[...] = grad[:taps]

    def own_spectra(array):
        def body(high, low, ref, *outs):
            for block in range(2):
                outs[block][...] = spectrum(high, low, ref[block * taps : (block + 1) * taps])

        return call(body, [struct(2 * taps, width, f32)] * 2, [*fwd, array])

    def lags(place_ref, inv_high, inv_low, p0, p1, g0, g1, behind, *refs):
        outs, full = refs[:-1], refs[-1]
        one = times_conj(parts(g0[...]), window(p0[...], behind[...], 1.0))
        two = times_conj(parts(g1[...]), window(p1[...], p0[...], 1.0))
        full[...] = restore(inv_high, inv_low, one[0] + two[0], one[1] + two[1])
        for step in range(planes):
            block = full[block_at(place_ref[1] ^ step, plane_taps)]
            outs[step][...] = block.astype(outs[step].dtype)

    def mix(place_ref, high, low, lag_high, lag_low, inv_high, inv_low, p0, p1, halo, *refs):
        keep, near, far, spec, spec_behind, own, side, ship, filt, mixed = refs
        q = place_ref[0]
        filt[block_at(q, column)] = keep[:column]
        filt[block_at(q ^ 1, column)] = near[:column]
        filt[block_at(q ^ 2, column)] = far[:column]
        filt[block_at(q ^ 3, column)] = far[column:]
        taps_spec = spectrum(lag_high, lag_low, filt[...])
        spec[...] = taps_spec
        spec_behind[...] = spectrum(high, low, halo[...])
        behind = (spec_behind, p0, p1)
        for block in range(2):
            value = times(parts(taps_spec), window(behind[block + 1][...], behind[block][...], 1.0))
            at = slice(block * taps, (block + 1) * taps)
            mixed[at] = restore(inv_high, inv_low, *value).astype(bf16)
        split(q, mixed, own, side, ship)

    def pick(ref, index):
        if own_taps % 8 == 0:
            return ref[block_at(index, own_taps)]
        value = ref[:own_taps]
        for n in range(1, PLANE):
            value = jnp.where(index == n, ref[n * own_taps : (n + 1) * own_taps], value)
        return value

    def split(q, source, own, side, ship):
        own[...] = source[block_at(q, rows)]
        side[...] = source[block_at(q ^ 1, rows)]
        ship[:rows] = source[block_at(q ^ 2, rows)]
        ship[rows:] = source[block_at(q ^ 3, rows)]

    def correlate(place_ref, high, low, inv_high, inv_low, g0, g1, halo, taps_ref, *refs):
        corr = refs[3]
        taps_spec = parts(taps_ref[...])
        ahead = (g0[...], g1[...], spectrum(high, low, halo[...]))
        for block in range(2):
            value = times_conj(window(ahead[block], ahead[block + 1], -1.0), taps_spec)
            at = slice(block * taps, (block + 1) * taps)
            corr[at] = restore(inv_high, inv_low, *value).astype(bf16)
        split(place_ref[0], corr, *refs[:3])

    def add_lags(place_ref, *refs):
        ins, outs, full = refs[:planes], refs[planes:-1], refs[-1]
        total = ins[0][...]
        for ref in ins[1:]:
            total = total + ref[...].astype(f32)
        full[...] = total * (1.0 / math.sqrt(rows * nseq))
        for step, out in enumerate(outs):
            out[...] = pick(full, place_ref[0] ^ step)

    def write(place_ref, blocks, gates, outs, held, sems):
        copies = []
        for step in range(PLANE):
            at = block_at(place_ref[0] ^ step, width)
            value = blocks[step].astype(f32)
            for n, (gate, out) in enumerate(zip(gates, outs)):
                held[n, step] = (value * gate[:, at].astype(f32)).astype(bf16)
                copy = pltpu.make_async_copy(held.at[n, step], out.at[:, at], sems.at[n, step])
                copy.start()
                copies.append(copy)
        return copies

    def finish_mixed(place_ref, own, near, far, o_ref, out, mark, held, sems):
        blocks = (own[...], near[:rows], far[:rows], near[rows:])
        copies = write(place_ref, blocks, [o_ref], [out], held, sems)
        mark[...] = jnp.zeros_like(mark)
        for copy in copies:
            copy.wait()

    def finish_corr(place_ref, own, near, far, v_ref, k_ref, *refs):
        lag_refs, (dk, dv, df, held, full, sems, sem) = refs[:PLANE], refs[PLANE:]
        q = place_ref[0]
        blocks = (own[...], near[:rows], far[:rows], near[rows:])
        copies = write(place_ref, blocks, [v_ref, k_ref], [dk, dv], held, sems)
        for step in range(PLANE):
            full[:, block_at(q ^ step, width)] = lag_refs[step][...]
        copy = pltpu.make_async_copy(full, df, sem)
        copy.start()
        for copy in copies + [copy]:
            copy.wait()

    block = struct(rows, width, bf16)
    double = struct(2 * rows, width, bf16)
    spectral = struct(2 * taps, width, f32)
    halo = struct(taps, width, bf16)

    def product_block(step):
        start = (place[0] ^ step) * width
        left = lax.dynamic_slice_in_dim(keys, start, width, 1).astype(f32)
        right = lax.dynamic_slice_in_dim(values, start, width, 1).astype(f32)
        return (left * right).astype(bf16)

    sent = [product_block(step) for step in range(PLANE)]
    far_p = [swap(sent[step], step) for step in (2, 3)]
    keep, side = call(
        gate_grad,
        [double, struct(3 * rows, width, bf16)],
        [place, out_grad, queries, sent[1]],
    )
    near = swap(side, 1)
    far = swap(join(keep, near), 2)

    (narrow,) = call(
        narrow_taps, [struct(pad_taps, channels, bf16)], [filter_taps], after=[near]
    )
    far_taps = [swap(narrow, PLANE * step) for step in range(1, planes)]
    taps_keep, taps_side = call(
        lay_taps,
        [struct(2 * column, width, bf16)] * 2,
        [place, narrow, *far_taps],
        scratch=[pltpu.VMEM((column, channels), bf16)],
        after=far_p,
    )
    taps_near = swap(taps_side, 1)
    (taps_ship,) = call(join_taps, [struct(2 * column, width, bf16)], [taps_keep, taps_near])
    taps_far = swap(taps_ship, 2)

    product, top = call(
        gather_product,
        [struct(tokens, width, bf16), halo],
        [place, sent[0], near, *far_p],
    )
    behind = shift(top, PLANE)
    p_spec = own_spectra(product)

    grad, bottom = call(
        gather_grad,
        [struct(tokens, width, bf16), halo],
        [place, keep, near, far],
        after=[taps_ship],
    )
    ahead = shift(bottom, -PLANE)
    g_spec = own_spectra(grad)

    taps_spec, behind_spec, own, side, ship = call(
        mix,
        [spectral, spectral, block, block, double],
        [place, *fwd, *fwd_lag, *inv, *p_spec, behind, taps_keep, taps_near, taps_far],
        scratch=[
            pltpu.VMEM((PLANE * column, width), bf16),
            pltpu.VMEM((tokens, width), bf16),
        ],
    )
    own_lags, *away = call(
        lags,
        [struct(plane_taps, width, f32)] + [struct(plane_taps, width, bf16)] * (planes - 1),
        [place, *inv, *p_spec, *g_spec, behind_spec],
        scratch=[pltpu.VMEM((taps, width), f32)],
    )
    far = swap(ship, 2)
    away = [swap(part, PLANE * (step + 1)) for step, part in enumerate(away)]
    corr_own, corr_side, corr_ship = call(
        correlate,
        [block, block, double],
        [place, *fwd, *inv, *g_spec, ahead, taps_spec],
        scratch=[pltpu.VMEM((tokens, width), bf16)],
        flops=LONG,
    )
    corr_far = swap(corr_ship, 2)
    near = swap(join(side, far, after=[corr_own]), 1)
    lag_blocks = call(
        add_lags,
        [struct(own_taps, width, f32)] * PLANE,
        [place, own_lags, *away],
        scratch=[pltpu.VMEM((plane_taps, width), f32)],
        after=[corr_own],
        flops=LONG,
    )
    lag_got = {step: swap(lag_blocks[step], step) for step in (2, 3, 1)}

    whole = struct(rows, channels, bf16)
    q_grad, mark = call(
        finish_mixed,
        [whole, struct(8, 128, f32)],
        [place, own, near, far, out_grad],
        scratch=[
            pltpu.VMEM((1, PLANE, rows, width), bf16),
            pltpu.SemaphoreType.DMA((1, PLANE)),
        ],
        spaces=[pl.ANY, pltpu.VMEM],
    )
    corr_near = swap(join(corr_side, corr_far, after=[mark, lag_blocks[0]]), 1)
    k_grad, v_grad, filter_grad = call(
        finish_corr,
        [whole, whole, struct(own_taps, channels, f32)],
        [place, corr_own, corr_near, corr_far, values, keys, lag_blocks[0]]
        + [lag_got[step] for step in range(1, PLANE)],
        scratch=[
            pltpu.VMEM((2, PLANE, rows, width), bf16),
            pltpu.VMEM((own_taps, channels), f32),
            pltpu.SemaphoreType.DMA((2, PLANE)),
            pltpu.SemaphoreType.DMA,
        ],
        spaces=[pl.ANY] * 3,
    )
    return (q_grad, k_grad, v_grad, filter_grad)


def solution(mesh):
    placed = (
        P(("grp", "seq"), None),
        P(("grp", "seq"), None),
        P(("grp", "seq"), None),
        P(("grp", "seq"), None),
        P("seq", None),
    )
    return jax.shard_map(
        shards,
        mesh=mesh,
        in_specs=placed,
        out_specs=(
            P(("grp", "seq"), None),
            P(("grp", "seq"), None),
            P(("grp", "seq"), None),
            P(("grp", "seq"), None),
        ),
        check_vma=False,
    )
```

```python
import math

import jax
import jax.numpy as jnp
import numpy as np
from jax import lax
from jax.experimental import pallas as pl
from jax.experimental.pallas import tpu as pltpu
from jax.sharding import PartitionSpec as P

PLANE = 4
VMEM_BYTES = 32 * 1024 * 1024


def tables(block):
    half = np.concatenate([np.arange(0, block, 2), np.arange(1, block, 2)])
    angle = np.pi * (half[:, None] + 0.5) * np.arange(block)[None, :] / block
    forward = np.concatenate([np.cos(angle), -np.sin(angle)], 0)
    inverse = forward.T / block
    return forward, inverse


def pair(table):
    high = table.astype(np.float32).astype(jnp.bfloat16)
    low = (table - high.astype(np.float64)).astype(np.float32).astype(jnp.bfloat16)
    return jnp.asarray(high), jnp.asarray(low)


def dot(left, right):
    return jnp.dot(left, right, preferred_element_type=jnp.float32)


def spectrum(high, low, block):
    return dot(high[...], block) + dot(low[...], block)


def restore(high, low, real, imag):
    spec = jnp.concatenate([real, imag], 0)
    top = spec.astype(jnp.bfloat16)
    rest = (spec - top.astype(jnp.float32)).astype(jnp.bfloat16)
    return dot(high[...], top) + dot(low[...], top) + dot(high[...], rest)


def parts(spec):
    half = spec.shape[0] // 2
    return spec[:half], spec[half:]


def turned(spec, sign):
    real, imag = parts(spec)
    quarter = real.shape[0] // 2
    flip = lambda a, s: jnp.concatenate([s * a[:quarter], -s * a[quarter:]], 0)
    return flip(imag, -sign), flip(real, sign)


def window(near, far, sign):
    real, imag = parts(near)
    other_real, other_imag = turned(far, sign)
    return real + other_real, imag + other_imag


def times(left, right):
    return left[0] * right[0] - left[1] * right[1], left[0] * right[1] + left[1] * right[0]


def times_conj(left, right):
    return left[0] * right[0] + left[1] * right[1], left[1] * right[0] - left[0] * right[1]


def call(body, outs, args, scratch=(), spaces=None, after=(), flops=1, aliases=()):
    specs = [
        pl.BlockSpec(memory_space=pltpu.SMEM if a.ndim == 1 else pltpu.VMEM) for a in args
    ]
    after = [*after, *aliases]
    specs += [pl.BlockSpec(memory_space=pl.ANY)] * len(after)
    base = len(args) + len(after) - len(aliases)

    def run(*refs):
        body(*refs[: len(args)], *refs[len(args) + len(after) :])

    spaces = spaces or [pltpu.VMEM] * len(outs)
    return pl.pallas_call(
        run,
        out_shape=outs,
        in_specs=specs,
        out_specs=[pl.BlockSpec(memory_space=space) for space in spaces],
        scratch_shapes=scratch,
        input_output_aliases={base + n: n for n in range(len(aliases))},
        compiler_params=pltpu.CompilerParams(vmem_limit_bytes=VMEM_BYTES),
        cost_estimate=pl.CostEstimate(flops=flops, bytes_accessed=1, transcendentals=0),
    )(*args, *after)


def shards(queries, keys, values, out_grad, filter_taps):
    f32, bf16 = jnp.float32, jnp.bfloat16
    rows, channels = queries.shape
    nseq = lax.axis_size("seq")
    own_taps = filter_taps.shape[0]
    taps = own_taps * nseq
    planes = nseq // PLANE
    width = channels // PLANE
    tokens = rows * PLANE
    pad_taps = max(16, own_taps)
    plane_taps = taps // planes
    column = planes * pad_taps
    assert tokens == 2 * taps
    me = lax.axis_index("seq")
    place = jnp.stack([me % PLANE, me // PLANE]).astype(jnp.int32)
    devices = range(nseq)

    forward, inverse = tables(taps)
    fwd = pair(forward)
    inv = pair(inverse)
    lag_of = np.full((planes * PLANE, pad_taps), -1)
    lag_of[:, :own_taps] = np.arange(taps).reshape(planes * PLANE, own_taps)
    lag_of = lag_of.reshape(planes, PLANE, pad_taps).transpose(1, 0, 2).reshape(-1)
    fwd_lag = pair(np.where(lag_of[None, :] >= 0, forward[:, np.maximum(lag_of, 0)], 0.0))

    def swap(array, distance):
        return lax.ppermute(array, "seq", [(i, i ^ distance) for i in devices])

    def shift(array, distance):
        return lax.ppermute(
            array, "seq", [(i, i + distance) for i in devices if i + distance in devices]
        )

    def struct(r, c, dtype):
        return jax.ShapeDtypeStruct((r, c), dtype)

    def block_at(index, size):
        return pl.ds(pl.multiple_of(index * size, size), size)

    def lay_taps(place_ref, *refs):
        ins, (keep, side, full) = refs[:planes], refs[planes:]
        q, z = place_ref[0], place_ref[1]
        for step in range(planes):
            full[block_at(z ^ step, pad_taps)] = ins[step][...]
        for step, (out, half) in enumerate(((keep, 0), (side, 0), (keep, 1), (side, 1))):
            out[half * column : (half + 1) * column] = full[:, block_at(q ^ step, width)]

    def narrow_taps(taps_ref, out):
        out[:own_taps] = taps_ref[...].astype(bf16)
        if pad_taps > own_taps:
            out[own_taps:] = jnp.zeros((pad_taps - own_taps, channels), bf16)

    def gate_grad(place_ref, o_ref, q_ref, p_ref, keep, side):
        q = place_ref[0]
        side[:rows] = p_ref[...]
        for step, (out, first) in enumerate(((keep, 0), (side, rows), (keep, rows), (side, 2 * rows))):
            at = block_at(q ^ step, width)
            out[first : first + rows] = (
                o_ref[:, at].astype(f32) * q_ref[:, at].astype(f32)
            ).astype(bf16)

    def join(left, right, after=(), flops=1):
        def body(left_ref, right_ref, out):
            out[:rows] = left_ref[left.shape[0] - rows :]
            out[rows:] = right_ref[right.shape[0] - rows :]

        return call(body, [struct(2 * rows, width, bf16)], [left, right], after=after, flops=flops)[0]

    def gather_product(place_ref, *refs):
        ins, (product, top) = refs[:PLANE], refs[PLANE:]
        q = place_ref[0]
        for step in range(PLANE):
            product[block_at(q ^ step, rows)] = ins[step][:rows]
        top[...] = product[tokens - taps :]

    def join_taps(keep, near, ship):
        ship[:column] = keep[column:]
        ship[column:] = near[column:]

    def gather_grad(place_ref, keep, near, far, grad, bottom):
        q = place_ref[0]
        grad[block_at(q, rows)] = keep[:rows]
        grad[block_at(q ^ 1, rows)] = near[rows : 2 * rows]
        grad[block_at(q ^ 2, rows)] = far[:rows]
        grad[block_at(q ^ 3, rows)] = far[rows:]
        bottom[...] = grad[:taps]

    def own_spectra(array, flops, after):
        def body(high, low, ref, *outs):
            for block in range(2):
                outs[block][...] = spectrum(high, low, ref[block * taps : (block + 1) * taps])

        return call(body, [struct(2 * taps, width, f32)] * 2, [*fwd, array], flops=flops, after=after)

    def lags(place_ref, high, low, inv_high, inv_low, p0, p1, g0, g1, halo, *refs):
        spec, outs, full = refs[0], refs[1:-1], refs[-1]
        behind = spectrum(high, low, halo[...])
        spec[...] = behind
        one = times_conj(parts(g0[...]), window(p0[...], behind, 1.0))
        two = times_conj(parts(g1[...]), window(p1[...], p0[...], 1.0))
        full[...] = restore(inv_high, inv_low, one[0] + two[0], one[1] + two[1])
        for step in range(planes):
            block = full[block_at(place_ref[1] ^ step, plane_taps)]
            outs[step][...] = block.astype(outs[step].dtype)

    def signal(inv_refs, taps_spec, near, far, sign):
        real, imag = parts(taps_spec)
        value = times((real, sign * imag), window(near, far, sign))
        return restore(*inv_refs, *value).astype(bf16)

    def inner(place_ref, high, low, inv_high, inv_low, p0, p1, g0, g1, *refs):
        keep, near_taps, far_taps, spec, ship, filt, held = refs
        q = place_ref[0]
        filt[block_at(q, column)] = keep[:column]
        filt[block_at(q ^ 1, column)] = near_taps[:column]
        filt[block_at(q ^ 2, column)] = far_taps[:column]
        filt[block_at(q ^ 3, column)] = far_taps[column:]
        taps_spec = spectrum(high, low, filt[...])
        spec[...] = taps_spec
        left = q < 2
        near = jnp.where(left, p1[...], g0[...])
        far = jnp.where(left, p0[...], g1[...])
        held[...] = signal((inv_high, inv_low), taps_spec, near, far, jnp.where(left, 1.0, -1.0))
        ship[:rows] = held[block_at(q % 2, rows)]
        ship[rows:] = held[block_at(1 - q % 2, rows)]

    def outer(place_ref, high, low, inv_high, inv_low, p0, g1, behind, halo, taps_ref, *refs):
        spec, ship, held = refs
        q = place_ref[0]
        ahead = spectrum(high, low, halo[...])
        spec[...] = ahead
        left = q < 2
        near = jnp.where(left, g1[...], p0[...])
        far = jnp.where(left, ahead, behind[...])
        sign = jnp.where(left, -1.0, 1.0)
        held[...] = signal((inv_high, inv_low), taps_ref[...], near, far, sign)
        ship[:rows] = held[block_at(q % 2, rows)]
        ship[rows:] = held[block_at(1 - q % 2, rows)]

    def kept(place_ref, inv_high, inv_low, p0, p1, g0, g1, behind, ahead, taps_ref, *refs):
        mixed_own, corr_own, side, held = refs
        q = place_ref[0]
        left = q < 2
        inv_refs = (inv_high, inv_low)
        near = jnp.where(left, p0[...], p1[...])
        far = jnp.where(left, behind[...], p0[...])
        held[...] = signal(inv_refs, taps_ref[...], near, far, 1.0)
        mixed_own[...] = held[block_at(q % 2, rows)]
        side[:rows] = held[block_at(1 - q % 2, rows)]
        near = jnp.where(left, g0[...], g1[...])
        far = jnp.where(left, g1[...], ahead[...])
        held[...] = signal(inv_refs, taps_ref[...], near, far, -1.0)
        corr_own[...] = held[block_at(q % 2, rows)]
        side[rows:] = held[block_at(1 - q % 2, rows)]

    def pick(ref, index):
        if own_taps % 8 == 0:
            return ref[block_at(index, own_taps)]
        value = ref[:own_taps]
        for n in range(1, PLANE):
            value = jnp.where(index == n, ref[n * own_taps : (n + 1) * own_taps], value)
        return value

    def add_lags(place_ref, *refs):
        ins, (own, side, ship, full) = refs[:planes], refs[planes:]
        q = place_ref[0]
        total = ins[0][...]
        for ref in ins[1:]:
            total = total + ref[...].astype(f32)
        full[...] = total * (1.0 / math.sqrt(rows * nseq))
        own[...] = pick(full, q)
        side[...] = pick(full, q ^ 1)
        ship[:own_taps] = pick(full, q ^ 2)
        ship[own_taps:] = pick(full, q ^ 3)

    def join_first(side, far, out):
        out[: 2 * rows] = side[...]
        out[2 * rows :] = far[rows:]

    def join_second(far, lag_side, lag_far, out, lag_out):
        out[...] = far[rows:]
        lag_out[:own_taps] = lag_side[...]
        lag_out[own_taps:] = lag_far[own_taps:]

    def write(place_ref, steps, values, gates, outs, held, sems):
        copies = []
        for n, step in enumerate(steps):
            at = block_at(place_ref[0] ^ step, width)
            for m, (gate, out) in enumerate(zip(gates, outs)):
                value = values[n][min(m, 1)].astype(f32)
                held[m, n] = (value * gate[:, at].astype(f32)).astype(bf16)
                copy = pltpu.make_async_copy(held.at[m, n], out.at[:, at], sems.at[m, n])
                copy.start()
                copies.append(copy)
        return copies

    def finish_near(place_ref, mixed, corr, near, o_ref, v_ref, k_ref, *refs):
        outs, (mark, held, sems) = refs[:3], refs[3:]
        values = ((mixed[...], corr[...]), (near[:rows], near[rows : 2 * rows]))
        copies = write(place_ref, (0, 1), values, (o_ref, v_ref, k_ref), outs, held, sems)
        mark[...] = jnp.zeros_like(mark)
        for copy in copies:
            copy.wait()

    def finish_far(place_ref, first, second, near, last, o_ref, v_ref, k_ref, *refs):
        lag_own, lag_near, lag_far, dq, dk, dv, df, held, full, sems, sem = refs
        q = place_ref[0]
        left = q < 2
        values = []
        for one, two in ((first[:rows], second[:rows]), (near[2 * rows :], last[...])):
            values.append((jnp.where(left, two, one), jnp.where(left, one, two)))
        copies = write(place_ref, (2, 3), values, (o_ref, v_ref, k_ref), (dq, dk, dv), held, sems)
        full[:, block_at(q, width)] = lag_own[...]
        full[:, block_at(q ^ 1, width)] = lag_near[:own_taps]
        full[:, block_at(q ^ 2, width)] = lag_far[:own_taps]
        full[:, block_at(q ^ 3, width)] = lag_near[own_taps:]
        copy = pltpu.make_async_copy(full, df, sem)
        copy.start()
        for copy in copies + [copy]:
            copy.wait()

    block = struct(rows, width, bf16)
    double = struct(2 * rows, width, bf16)
    spectral = struct(2 * taps, width, f32)
    halo = struct(taps, width, bf16)

    def product_block(step):
        start = (place[0] ^ step) * width
        left = lax.dynamic_slice_in_dim(keys, start, width, 1).astype(f32)
        right = lax.dynamic_slice_in_dim(values, start, width, 1).astype(f32)
        return (left * right).astype(bf16)

    sent = [product_block(step) for step in range(PLANE)]
    far_p = [swap(sent[step], step) for step in (2, 3)]
    keep, side = call(
        gate_grad,
        flops=1,
        outs=[double, struct(3 * rows, width, bf16)],
        args=[place, out_grad, queries, sent[1]],
        after=[],
    )
    near = swap(side, 1)
    far = swap(join(keep, near, after=[far_p[1]], flops=1000000000), 2)

    product, top = call(
        gather_product,
        [struct(tokens, width, bf16), halo],
        [place, sent[0], near, *far_p],
        flops=1,
    )
    (narrow,) = call(
        narrow_taps,
        [struct(pad_taps, channels, bf16)],
        [filter_taps],
        after=[near],
        flops=1,
    )
    far_taps = [swap(narrow, PLANE * step) for step in range(1, planes)]
    taps_keep, taps_side = call(
        lay_taps,
        [struct(2 * column, width, bf16)] * 2,
        [place, narrow, *far_taps],
        scratch=[pltpu.VMEM((column, channels), bf16)],
        after=[product],
        flops=1,
    )
    taps_near = swap(taps_side, 1)
    (taps_ship,) = call(
        join_taps,
        [struct(2 * column, width, bf16)],
        [taps_keep, taps_near],
        flops=1,
    )
    taps_far = swap(taps_ship, 2)

    behind = shift(top, PLANE)
    p_spec = own_spectra(product, 1, [])

    grad, bottom = call(
        gather_grad,
        [struct(tokens, width, bf16), halo],
        [place, keep, near, far],
        after=[taps_ship],
        flops=1,
    )
    ahead = shift(bottom, -PLANE)
    g_spec = own_spectra(grad, 1, [])

    taps_spec, ship = call(
        inner,
        [spectral, double],
        [place, *fwd_lag, *inv, *p_spec, *g_spec, taps_keep, taps_near, taps_far],
        scratch=[pltpu.VMEM((PLANE * column, width), bf16), pltpu.VMEM((taps, width), bf16)],
        after=[],
        flops=10000000000,
    )
    first = swap(ship, 2)
    behind_spec, own_lags, *away = call(
        lags,
        [spectral, struct(plane_taps, width, f32)]
        + [struct(plane_taps, width, bf16)] * (planes - 1),
        [place, *fwd, *inv, *p_spec, *g_spec, behind],
        scratch=[pltpu.VMEM((taps, width), f32)],
        after=[taps_spec],
        flops=1,
    )
    away = [swap(part, PLANE * (step + 1)) for step, part in enumerate(away)]
    ahead_spec, ship = call(
        outer,
        [spectral, double],
        [place, *fwd, *inv, p_spec[0], g_spec[1], behind_spec, ahead, taps_spec],
        scratch=[pltpu.VMEM((taps, width), bf16)],
        after=[taps_spec],
        flops=1,
    )
    second = swap(ship, 2)
    mixed_own, corr_own, side = call(
        kept,
        [block, block, double],
        [place, *inv, *p_spec, *g_spec, behind_spec, ahead_spec, taps_spec],
        scratch=[pltpu.VMEM((taps, width), bf16)],
        after=[first],
        flops=1,
    )
    triple = struct(3 * rows, width, bf16)
    (joined,) = call(
        join_first, [triple], [side, first], after=[], flops=1
    )
    near = swap(joined, 1)
    lag_double = struct(2 * own_taps, width, f32)
    lag_own, lag_side, lag_ship = call(
        add_lags,
        [struct(own_taps, width, f32)] * 2 + [lag_double],
        [place, own_lags, *away],
        scratch=[pltpu.VMEM((plane_taps, width), f32)],
        after=[corr_own],
        flops=10000000000,
    )
    lag_far = swap(lag_ship, 2)
    whole = struct(rows, channels, bf16)
    *partial, mark = call(
        finish_near,
        [whole] * 3 + [struct(8, 128, f32)],
        [place, mixed_own, corr_own, near, out_grad, values, keys],
        scratch=[
            pltpu.VMEM((3, 2, rows, width), bf16),
            pltpu.SemaphoreType.DMA((3, 2)),
        ],
        spaces=[pl.ANY] * 3 + [pltpu.VMEM],
        flops=1,
    )
    joined, lag_joined = call(
        join_second,
        [block, lag_double],
        [second, lag_side, lag_far],
        after=[mark],
        flops=1,
    )
    last = swap(joined, 1)
    lag_near = swap(lag_joined, 1)
    return call(
        finish_far,
        [whole] * 3 + [struct(own_taps, channels, f32)],
        [place, first, second, near, last, out_grad, values, keys, lag_own, lag_near, lag_far],
        scratch=[
            pltpu.VMEM((3, 2, rows, width), bf16),
            pltpu.VMEM((own_taps, channels), f32),
            pltpu.SemaphoreType.DMA((3, 2)),
            pltpu.SemaphoreType.DMA,
        ],
        spaces=[pl.ANY] * 4,
        aliases=partial,
    )


def solution(mesh):
    placed = (
        P(("grp", "seq"), None),
        P(("grp", "seq"), None),
        P(("grp", "seq"), None),
        P(("grp", "seq"), None),
        P("seq", None),
    )
    return jax.shard_map(
        shards,
        mesh=mesh,
        in_specs=placed,
        out_specs=(
            P(("grp", "seq"), None),
            P(("grp", "seq"), None),
            P(("grp", "seq"), None),
            P(("grp", "seq"), None),
        ),
        check_vma=False,
    )
```

```python
import math

import jax
import jax.numpy as jnp
import numpy as np
from jax import lax
from jax.experimental import pallas as pl
from jax.experimental.pallas import tpu as pltpu
from jax.sharding import PartitionSpec as P

PLANE = 4
VMEM_BYTES = 32 * 1024 * 1024


def tables(block):
    half = np.concatenate([np.arange(0, block, 2), np.arange(1, block, 2)])
    angle = np.pi * (half[:, None] + 0.5) * np.arange(block)[None, :] / block
    forward = np.concatenate([np.cos(angle), -np.sin(angle)], 0)
    inverse = forward.T / block
    return forward, inverse


def pair(table):
    high = table.astype(np.float32).astype(jnp.bfloat16)
    low = (table - high.astype(np.float64)).astype(np.float32).astype(jnp.bfloat16)
    return jnp.asarray(high), jnp.asarray(low)


def dot(left, right):
    return jnp.dot(left, right, preferred_element_type=jnp.float32)


def spectrum(high, low, block):
    return dot(high[...], block) + dot(low[...], block)


def restore(high, low, real, imag):
    spec = jnp.concatenate([real, imag], 0)
    top = spec.astype(jnp.bfloat16)
    return dot(high[...], top) + dot(low[...], top)


def parts(spec):
    half = spec.shape[0] // 2
    return spec[:half], spec[half:]


def turned(spec, sign):
    real, imag = parts(spec)
    quarter = real.shape[0] // 2
    flip = lambda a, s: jnp.concatenate([s * a[:quarter], -s * a[quarter:]], 0)
    return flip(imag, -sign), flip(real, sign)


def window(near, far, sign):
    real, imag = parts(near)
    other_real, other_imag = turned(far, sign)
    return real + other_real, imag + other_imag


def times(left, right):
    return left[0] * right[0] - left[1] * right[1], left[0] * right[1] + left[1] * right[0]


def times_conj(left, right):
    return left[0] * right[0] + left[1] * right[1], left[1] * right[0] - left[0] * right[1]


class Here:
    def __getitem__(self, index):
        me = lax.axis_index("seq")
        return me // PLANE if index else me % PLANE


def call(body, outs, args, scratch=(), spaces=None, after=(), flops=1, aliases=()):
    located = args[0] is None
    args = args[1:] if located else args
    specs = [
        pl.BlockSpec(memory_space=pltpu.VMEM) for _ in args
    ]
    after = [*after, *aliases]
    specs += [pl.BlockSpec(memory_space=pl.ANY)] * len(after)
    base = len(args) + len(after) - len(aliases)

    def run(*refs):
        first = [Here()] if located else []
        body(*first, *refs[: len(args)], *refs[len(args) + len(after) :])

    spaces = spaces or [pltpu.VMEM] * len(outs)
    return pl.pallas_call(
        run,
        out_shape=outs,
        in_specs=specs,
        out_specs=[pl.BlockSpec(memory_space=space) for space in spaces],
        scratch_shapes=scratch,
        input_output_aliases={base + n: n for n in range(len(aliases))},
        compiler_params=pltpu.CompilerParams(vmem_limit_bytes=VMEM_BYTES),
        cost_estimate=pl.CostEstimate(flops=flops, bytes_accessed=1, transcendentals=0),
    )(*args, *after)


def shards(queries, keys, values, out_grad, filter_taps):
    f32, bf16 = jnp.float32, jnp.bfloat16
    rows, channels = queries.shape
    nseq = lax.axis_size("seq")
    own_taps = filter_taps.shape[0]
    taps = own_taps * nseq
    planes = nseq // PLANE
    width = channels // PLANE
    tokens = rows * PLANE
    pad_taps = max(16, own_taps)
    plane_taps = taps // planes
    column = planes * pad_taps
    assert tokens == 2 * taps
    me = lax.axis_index("seq")
    devices = range(nseq)

    forward, inverse = tables(taps)
    fwd = pair(forward)
    inv = pair(inverse)
    lag_of = np.full((planes * PLANE, pad_taps), -1)
    lag_of[:, :own_taps] = np.arange(taps).reshape(planes * PLANE, own_taps)
    lag_of = lag_of.reshape(-1)
    if pad_taps == own_taps:
        fwd_lag = fwd
    else:
        fwd_lag = pair(np.where(lag_of[None, :] >= 0, forward[:, np.maximum(lag_of, 0)], 0.0))

    def swap(array, distance):
        return lax.ppermute(array, "seq", [(i, i ^ distance) for i in devices])

    def shift(array, distance):
        return lax.ppermute(
            array, "seq", [(i, i + distance) for i in devices if i + distance in devices]
        )

    def struct(r, c, dtype):
        return jax.ShapeDtypeStruct((r, c), dtype)

    def block_at(index, size):
        return pl.ds(pl.multiple_of(index * size, size), size)

    def lay_taps(place_ref, *refs):
        ins, (keep, ship) = refs[:planes], refs[planes:]
        q, z = place_ref[0], place_ref[1]
        for step in range(planes):
            for core in range(2):
                at = block_at(2 * (z ^ step) + (q % 2 ^ core), pad_taps)
                first = 2 * core * pad_taps
                keep[at] = ins[step][first : first + pad_taps]
                ship[at] = ins[step][first + pad_taps : first + 2 * pad_taps]

    def taps_block(taps_ref, at):
        block = taps_ref[:, at]
        if pad_taps > own_taps:
            fill = jnp.zeros((pad_taps - own_taps, width), f32)
            block = jnp.concatenate([block, fill], 0)
        return block.astype(bf16)

    def pack_taps(place_ref, taps_ref, near_ref, out):
        q = place_ref[0]
        out[:pad_taps] = taps_block(taps_ref, block_at(q, width))
        out[pad_taps : 2 * pad_taps] = taps_block(taps_ref, block_at(q ^ 2, width))
        out[2 * pad_taps :] = near_ref[3 * rows :]

    def gate_grad(place_ref, o_ref, q_ref, p_ref, taps_ref, keep, side):
        q = place_ref[0]
        side[:rows] = p_ref[...]
        for step, (out, first) in enumerate(((keep, 0), (side, rows), (keep, rows), (side, 2 * rows))):
            at = block_at(q ^ step, width)
            out[first : first + rows] = (
                o_ref[:, at].astype(f32) * q_ref[:, at].astype(f32)
            ).astype(bf16)
        for n, step in enumerate((1, 3)):
            first = 3 * rows + n * pad_taps
            side[first : first + pad_taps] = taps_block(taps_ref, block_at(q ^ step, width))

    def join(left, right, after=(), flops=1):
        def body(left_ref, right_ref, out):
            out[:rows] = left_ref[rows : 2 * rows]
            out[rows:] = right_ref[2 * rows : 3 * rows]

        return call(body, [struct(2 * rows, width, bf16)], [left, right], after=after, flops=flops)[0]

    def gather_product(place_ref, *refs):
        ins, (product, top) = refs[:PLANE], refs[PLANE:]
        q = place_ref[0]
        for step in range(PLANE):
            product[block_at(q ^ step, rows)] = ins[step][:rows]
        top[...] = product[tokens - taps :]

    def gather_grad(place_ref, keep, near, far, grad, bottom):
        q = place_ref[0]
        grad[block_at(q, rows)] = keep[:rows]
        grad[block_at(q ^ 1, rows)] = near[rows : 2 * rows]
        grad[block_at(q ^ 2, rows)] = far[:rows]
        grad[block_at(q ^ 3, rows)] = far[rows:]
        bottom[...] = grad[:taps]

    def own_spectra(array, flops, after):
        def body(high, low, ref, *outs):
            for block in range(2):
                outs[block][...] = spectrum(high, low, ref[block * taps : (block + 1) * taps])

        return call(body, [struct(2 * taps, width, f32)] * 2, [*fwd, array], flops=flops, after=after)

    def lags(place_ref, high, low, inv_high, inv_low, p0, p1, g0, g1, halo, *refs):
        spec, outs, full = refs[0], refs[1:-1], refs[-1]
        behind = spectrum(high, low, halo[...])
        spec[...] = behind
        one = times_conj(parts(g0[...]), window(p0[...], behind, 1.0))
        two = times_conj(parts(g1[...]), window(p1[...], p0[...], 1.0))
        full[...] = restore(inv_high, inv_low, one[0] + two[0], one[1] + two[1])
        for step in range(planes):
            block = full[block_at(place_ref[1] ^ step, plane_taps)]
            outs[step][...] = block.astype(outs[step].dtype)

    def mixed_of(inv_refs, taps_spec, near, far):
        value = times(parts(taps_spec), window(near[...], far[...], 1.0))
        return restore(*inv_refs, *value).astype(bf16)

    def corr_of(inv_refs, taps_spec, near, far):
        value = times_conj(window(near[...], far[...], -1.0), parts(taps_spec))
        return restore(*inv_refs, *value).astype(bf16)

    def by_side(q, left, right):
        pl.when(q < 2)(left)
        pl.when(q >= 2)(right)

    def inner(place_ref, high, low, inv_high, inv_low, p0, p1, g0, g1, *refs):
        keep, far_taps, spec, ship, filt, held = refs
        q = place_ref[0]
        chip = 2 * pad_taps
        for z in range(planes):
            at = slice(z * chip, (z + 1) * chip)
            filt[block_at(2 * z + q // 2, chip)] = keep[at]
            filt[block_at(2 * z + 1 - q // 2, chip)] = far_taps[at]
        taps_spec = spectrum(high, low, filt[...])
        spec[...] = taps_spec
        inv_refs = (inv_high, inv_low)

        def left():
            held[...] = mixed_of(inv_refs, spec[...], p1, p0)

        def right():
            held[...] = corr_of(inv_refs, spec[...], g0, g1)

        by_side(q, left, right)
        ship[:rows] = held[block_at(q % 2, rows)]
        ship[rows:] = held[block_at(1 - q % 2, rows)]

    def outer(place_ref, high, low, inv_high, inv_low, p0, g1, behind, halo, taps_ref, *refs):
        spec, ship, held = refs
        q = place_ref[0]
        ahead = spectrum(high, low, halo[...])
        spec[...] = ahead
        inv_refs = (inv_high, inv_low)

        def left():
            held[...] = corr_of(inv_refs, taps_ref[...], g1, spec)

        def right():
            held[...] = mixed_of(inv_refs, taps_ref[...], p0, behind)

        by_side(q, left, right)
        ship[:rows] = held[block_at(q % 2, rows)]
        ship[rows:] = held[block_at(1 - q % 2, rows)]

    def kept(place_ref, inv_high, inv_low, p0, p1, g0, g1, behind, ahead, taps_ref, *refs):
        mixed_own, corr_own, side, held = refs
        q = place_ref[0]
        inv_refs = (inv_high, inv_low)

        def run(p_near, p_far, g_near, g_far):
            held[...] = mixed_of(inv_refs, taps_ref[...], p_near, p_far)
            mixed_own[...] = held[block_at(q % 2, rows)]
            side[:rows] = held[block_at(1 - q % 2, rows)]
            held[...] = corr_of(inv_refs, taps_ref[...], g_near, g_far)
            corr_own[...] = held[block_at(q % 2, rows)]
            side[rows:] = held[block_at(1 - q % 2, rows)]

        by_side(q, lambda: run(p0, behind, g0, g1), lambda: run(p1, p0, g1, ahead))

    def pick(ref, index):
        if own_taps % 8 == 0:
            return ref[block_at(index, own_taps)]
        value = ref[:own_taps]
        for n in range(1, PLANE):
            value = jnp.where(index == n, ref[n * own_taps : (n + 1) * own_taps], value)
        return value

    def add_lags(place_ref, *refs):
        ins, (own, side, ship, full) = refs[:planes], refs[planes:]
        q = place_ref[0]
        total = ins[0][...]
        for ref in ins[1:]:
            total = total + ref[...].astype(f32)
        full[...] = total * (1.0 / math.sqrt(rows * nseq))
        own[...] = pick(full, q)
        side[...] = pick(full, q ^ 1)
        ship[:own_taps] = pick(full, q ^ 2)
        ship[own_taps:] = pick(full, q ^ 3)

    def join_first(side, far, out):
        out[: 2 * rows] = side[...]
        out[2 * rows :] = far[rows:]

    def join_second(far, lag_side, lag_far, out, lag_out):
        out[...] = far[rows:]
        lag_out[:own_taps] = lag_side[...]
        lag_out[own_taps:] = lag_far[own_taps:]

    def write(place_ref, steps, values, gates, outs, held, sems):
        copies = []
        for n, step in enumerate(steps):
            at = block_at(place_ref[0] ^ step, width)
            for m, (gate, out) in enumerate(zip(gates, outs)):
                value = values[n][min(m, 1)].astype(f32)
                held[m, n] = (value * gate[:, at].astype(f32)).astype(bf16)
                copy = pltpu.make_async_copy(held.at[m, n], out.at[:, at], sems.at[m, n])
                copy.start()
                copies.append(copy)
        return copies

    def finish_near(place_ref, mixed, corr, near, o_ref, v_ref, k_ref, *refs):
        outs, (mark, held, sems) = refs[:3], refs[3:]
        values = ((mixed[...], corr[...]), (near[:rows], near[rows : 2 * rows]))
        copies = write(place_ref, (0, 1), values, (o_ref, v_ref, k_ref), outs, held, sems)
        mark[...] = jnp.zeros_like(mark)
        for copy in copies:
            copy.wait()

    def finish_far(place_ref, first, second, near, last, o_ref, v_ref, k_ref, *refs):
        lag_own, lag_near, lag_far, dq, dk, dv, df, held, full, sems, sem = refs
        q = place_ref[0]
        left = q < 2
        values = []
        for one, two in ((first[:rows], second[:rows]), (near[2 * rows :], last[...])):
            values.append((jnp.where(left, two, one), jnp.where(left, one, two)))
        copies = write(place_ref, (2, 3), values, (o_ref, v_ref, k_ref), (dq, dk, dv), held, sems)
        full[:, block_at(q, width)] = lag_own[...]
        full[:, block_at(q ^ 1, width)] = lag_near[:own_taps]
        full[:, block_at(q ^ 2, width)] = lag_far[:own_taps]
        full[:, block_at(q ^ 3, width)] = lag_near[own_taps:]
        copy = pltpu.make_async_copy(full, df, sem)
        copy.start()
        for copy in copies + [copy]:
            copy.wait()

    block = struct(rows, width, bf16)
    double = struct(2 * rows, width, bf16)
    spectral = struct(2 * taps, width, f32)
    halo = struct(taps, width, bf16)

    def product_block(step):
        start = (me % PLANE ^ step) * width
        left = lax.dynamic_slice_in_dim(keys, start, width, 1).astype(f32)
        right = lax.dynamic_slice_in_dim(values, start, width, 1).astype(f32)
        return (left * right).astype(bf16)

    sent = [product_block(step) for step in range(PLANE)]
    far_p = [swap(sent[step], step) for step in (2, 3)]
    keep, side = call(
        gate_grad,
        flops=1,
        outs=[double, struct(3 * rows + 2 * pad_taps, width, bf16)],
        args=[None, out_grad, queries, sent[1], filter_taps],
        after=[],
    )
    near = swap(side, 1)

    product, top = call(
        gather_product,
        [struct(tokens, width, bf16), halo],
        [None, sent[0], near, *far_p],
        flops=1,
    )
    p_spec = own_spectra(product, 1, [])
    (packed,) = call(
        pack_taps,
        [struct(4 * pad_taps, width, bf16)],
        [None, filter_taps, near],
        after=[],
        flops=1,
    )
    far_taps = [swap(packed, PLANE * step) for step in range(1, planes)]
    far = swap(join(keep, near, after=[], flops=1000000000), 2)
    taps_keep, taps_ship = call(
        lay_taps,
        [struct(2 * column, width, bf16)] * 2,
        [None, packed, *far_taps],
        after=[p_spec[0]],
        flops=1000000000,
    )
    taps_far = swap(taps_ship, 2)

    behind = shift(top, PLANE)

    grad, bottom = call(
        gather_grad,
        [struct(tokens, width, bf16), halo],
        [None, keep, near, far],
        after=[taps_ship],
        flops=1,
    )
    ahead = shift(bottom, -PLANE)
    g_spec = own_spectra(grad, 1, [])

    taps_spec, ship = call(
        inner,
        [spectral, double],
        [None, *fwd_lag, *inv, *p_spec, *g_spec, taps_keep, taps_far],
        scratch=[pltpu.VMEM((PLANE * column, width), bf16), pltpu.VMEM((taps, width), bf16)],
        after=[],
        flops=1,
    )
    first = swap(ship, 2)
    behind_spec, own_lags, *away = call(
        lags,
        [spectral, struct(plane_taps, width, f32)]
        + [struct(plane_taps, width, bf16)] * (planes - 1),
        [None, *fwd, *inv, *p_spec, *g_spec, behind],
        scratch=[pltpu.VMEM((taps, width), f32)],
        after=[taps_spec],
        flops=1,
    )
    away = [swap(part, PLANE * (step + 1)) for step, part in enumerate(away)]
    ahead_spec, ship = call(
        outer,
        [spectral, double],
        [None, *fwd, *inv, p_spec[0], g_spec[1], behind_spec, ahead, taps_spec],
        scratch=[pltpu.VMEM((taps, width), bf16)],
        after=[taps_spec],
        flops=1,
    )
    second = swap(ship, 2)
    mixed_own, corr_own, side = call(
        kept,
        [block, block, double],
        [None, *inv, *p_spec, *g_spec, behind_spec, ahead_spec, taps_spec],
        scratch=[pltpu.VMEM((taps, width), bf16)],
        after=[first],
        flops=1,
    )
    triple = struct(3 * rows, width, bf16)
    (joined,) = call(
        join_first, [triple], [side, first], after=[], flops=1
    )
    near = swap(joined, 1)
    lag_double = struct(2 * own_taps, width, f32)
    lag_own, lag_side, lag_ship = call(
        add_lags,
        [struct(own_taps, width, f32)] * 2 + [lag_double],
        [None, own_lags, *away],
        scratch=[pltpu.VMEM((plane_taps, width), f32)],
        after=[corr_own],
        flops=10000000000,
    )
    lag_far = swap(lag_ship, 2)
    whole = struct(rows, channels, bf16)
    *partial, mark = call(
        finish_near,
        [whole] * 3 + [struct(8, 128, f32)],
        [None, mixed_own, corr_own, near, out_grad, values, keys],
        scratch=[
            pltpu.VMEM((3, 2, rows, width), bf16),
            pltpu.SemaphoreType.DMA((3, 2)),
        ],
        spaces=[pl.ANY] * 3 + [pltpu.VMEM],
        flops=1,
    )
    joined, lag_joined = call(
        join_second,
        [block, lag_double],
        [second, lag_side, lag_far],
        after=[mark],
        flops=1,
    )
    last = swap(joined, 1)
    lag_near = swap(lag_joined, 1)
    return call(
        finish_far,
        [whole] * 3 + [struct(own_taps, channels, f32)],
        [None, first, second, near, last, out_grad, values, keys, lag_own, lag_near, lag_far],
        scratch=[
            pltpu.VMEM((3, 2, rows, width), bf16),
            pltpu.VMEM((own_taps, channels), f32),
            pltpu.SemaphoreType.DMA((3, 2)),
            pltpu.SemaphoreType.DMA,
        ],
        spaces=[pl.ANY] * 4,
        aliases=partial,
    )


def solution(mesh):
    placed = (
        P(("grp", "seq"), None),
        P(("grp", "seq"), None),
        P(("grp", "seq"), None),
        P(("grp", "seq"), None),
        P("seq", None),
    )
    return jax.shard_map(
        shards,
        mesh=mesh,
        in_specs=placed,
        out_specs=(
            P(("grp", "seq"), None),
            P(("grp", "seq"), None),
            P(("grp", "seq"), None),
            P(("grp", "seq"), None),
        ),
        check_vma=False,
    )
```

```python
import math

import jax
import jax.numpy as jnp
import numpy as np
from jax import lax
from jax.experimental import pallas as pl
from jax.experimental.pallas import tpu as pltpu
from jax.sharding import PartitionSpec as P

PLANE = 4
VMEM_BYTES = 32 * 1024 * 1024


def tables(block):
    half = np.concatenate([np.arange(0, block, 2), np.arange(1, block, 2)])
    angle = np.pi * (half[:, None] + 0.5) * np.arange(block)[None, :] / block
    forward = np.concatenate([np.cos(angle), -np.sin(angle)], 0)
    inverse = forward.T / block
    return forward, inverse


def pair(table):
    high = table.astype(np.float32).astype(jnp.bfloat16)
    low = (table - high.astype(np.float64)).astype(np.float32).astype(jnp.bfloat16)
    return jnp.asarray(high), jnp.asarray(low)


def dot(left, right):
    return jnp.dot(left, right, preferred_element_type=jnp.float32)


def spectrum(high, low, block):
    return dot(high[...], block) + dot(low[...], block)


def restore(high, low, real, imag):
    spec = jnp.concatenate([real, imag], 0)
    top = spec.astype(jnp.bfloat16)
    return dot(high[...], top) + dot(low[...], top)


def parts(spec):
    half = spec.shape[0] // 2
    return spec[:half], spec[half:]


def turned(spec, sign):
    real, imag = parts(spec)
    quarter = real.shape[0] // 2
    flip = lambda a, s: jnp.concatenate([s * a[:quarter], -s * a[quarter:]], 0)
    return flip(imag, -sign), flip(real, sign)


def window(near, far, sign):
    real, imag = parts(near)
    other_real, other_imag = turned(far, sign)
    return real + other_real, imag + other_imag


def times(left, right):
    return left[0] * right[0] - left[1] * right[1], left[0] * right[1] + left[1] * right[0]


def times_conj(left, right):
    return left[0] * right[0] + left[1] * right[1], left[1] * right[0] - left[0] * right[1]


class Here:
    def __getitem__(self, index):
        me = lax.axis_index("seq")
        return me // PLANE if index else me % PLANE


def call(body, outs, args, scratch=(), spaces=None, after=(), flops=1, aliases=()):
    located = args[0] is None
    args = args[1:] if located else args
    specs = [
        pl.BlockSpec(memory_space=pltpu.VMEM) for _ in args
    ]
    after = [*after, *aliases]
    specs += [pl.BlockSpec(memory_space=pl.ANY)] * len(after)
    base = len(args) + len(after) - len(aliases)

    def run(*refs):
        first = [Here()] if located else []
        body(*first, *refs[: len(args)], *refs[len(args) + len(after) :])

    spaces = spaces or [pltpu.VMEM] * len(outs)
    return pl.pallas_call(
        run,
        out_shape=outs,
        in_specs=specs,
        out_specs=[pl.BlockSpec(memory_space=space) for space in spaces],
        scratch_shapes=scratch,
        input_output_aliases={base + n: n for n in range(len(aliases))},
        compiler_params=pltpu.CompilerParams(vmem_limit_bytes=VMEM_BYTES),
        cost_estimate=pl.CostEstimate(flops=flops, bytes_accessed=1, transcendentals=0),
    )(*args, *after)


def shards(queries, keys, values, out_grad, filter_taps):
    f32, bf16 = jnp.float32, jnp.bfloat16
    rows, channels = queries.shape
    nseq = lax.axis_size("seq")
    own_taps = filter_taps.shape[0]
    taps = own_taps * nseq
    planes = nseq // PLANE
    width = channels // PLANE
    tokens = rows * PLANE
    pad_taps = max(16, own_taps)
    plane_taps = taps // planes
    column = planes * pad_taps
    assert tokens == 2 * taps
    me = lax.axis_index("seq")
    devices = range(nseq)

    forward, inverse = tables(taps)
    fwd = pair(forward)
    inv = pair(inverse)
    lag_of = np.full((planes * PLANE, pad_taps), -1)
    lag_of[:, :own_taps] = np.arange(taps).reshape(planes * PLANE, own_taps)
    lag_of = lag_of.reshape(-1)
    if pad_taps == own_taps:
        fwd_lag = fwd
    else:
        fwd_lag = pair(np.where(lag_of[None, :] >= 0, forward[:, np.maximum(lag_of, 0)], 0.0))

    def swap(array, distance):
        return lax.ppermute(array, "seq", [(i, i ^ distance) for i in devices])

    def shift(array, distance):
        return lax.ppermute(
            array, "seq", [(i, i + distance) for i in devices if i + distance in devices]
        )

    def struct(r, c, dtype):
        return jax.ShapeDtypeStruct((r, c), dtype)

    def block_at(index, size):
        return pl.ds(pl.multiple_of(index * size, size), size)

    def lay_taps(place_ref, *refs):
        ins, (keep, ship) = refs[:planes], refs[planes:]
        q, z = place_ref[0], place_ref[1]
        for step in range(planes):
            for core in range(2):
                at = block_at(2 * (z ^ step) + (q % 2 ^ core), pad_taps)
                first = 2 * core * pad_taps
                keep[at] = ins[step][first : first + pad_taps]
                ship[at] = ins[step][first + pad_taps : first + 2 * pad_taps]

    def taps_block(taps_ref, at):
        block = taps_ref[:, at]
        if pad_taps > own_taps:
            fill = jnp.zeros((pad_taps - own_taps, width), f32)
            block = jnp.concatenate([block, fill], 0)
        return block.astype(bf16)

    def pack_taps(place_ref, taps_ref, near_ref, out):
        q = place_ref[0]
        out[:pad_taps] = taps_block(taps_ref, block_at(q, width))
        out[pad_taps : 2 * pad_taps] = taps_block(taps_ref, block_at(q ^ 2, width))
        out[2 * pad_taps :] = near_ref[3 * rows :]

    def gate_grad(place_ref, o_ref, q_ref, p_ref, taps_ref, keep, side):
        q = place_ref[0]
        side[:rows] = p_ref[...]
        for step, (out, first) in enumerate(((keep, 0), (side, rows), (keep, rows), (side, 2 * rows))):
            at = block_at(q ^ step, width)
            out[first : first + rows] = (
                o_ref[:, at].astype(f32) * q_ref[:, at].astype(f32)
            ).astype(bf16)
        for n, step in enumerate((1, 3)):
            first = 3 * rows + n * pad_taps
            side[first : first + pad_taps] = taps_block(taps_ref, block_at(q ^ step, width))

    def join(left, right, after=(), flops=1):
        def body(left_ref, right_ref, out):
            out[:rows] = left_ref[rows : 2 * rows]
            out[rows:] = right_ref[2 * rows : 3 * rows]

        return call(body, [struct(2 * rows, width, bf16)], [left, right], after=after, flops=flops)[0]

    def gather_product(place_ref, *refs):
        ins, (product, top) = refs[:PLANE], refs[PLANE:]
        q = place_ref[0]
        for step in range(PLANE):
            product[block_at(q ^ step, rows)] = ins[step][:rows]
        top[...] = product[tokens - taps :]

    def gather_grad(place_ref, keep, near, far, grad, bottom):
        q = place_ref[0]
        grad[block_at(q, rows)] = keep[:rows]
        grad[block_at(q ^ 1, rows)] = near[rows : 2 * rows]
        grad[block_at(q ^ 2, rows)] = far[:rows]
        grad[block_at(q ^ 3, rows)] = far[rows:]
        bottom[...] = grad[:taps]

    def own_spectra(array, flops, after):
        def body(high, low, ref, *outs):
            for block in range(2):
                outs[block][...] = spectrum(high, low, ref[block * taps : (block + 1) * taps])

        return call(body, [struct(2 * taps, width, f32)] * 2, [*fwd, array], flops=flops, after=after)

    def lags(place_ref, high, low, inv_high, inv_low, p0, p1, g0, g1, halo, *refs):
        spec, outs, full = refs[0], refs[1:-1], refs[-1]
        behind = spectrum(high, low, halo[...])
        spec[...] = behind
        one = times_conj(parts(g0[...]), window(p0[...], behind, 1.0))
        two = times_conj(parts(g1[...]), window(p1[...], p0[...], 1.0))
        full[...] = restore(inv_high, inv_low, one[0] + two[0], one[1] + two[1])
        for step in range(planes):
            block = full[block_at(place_ref[1] ^ step, plane_taps)]
            outs[step][...] = block.astype(outs[step].dtype)

    def mixed_of(inv_refs, taps_spec, near, far):
        value = times(parts(taps_spec), window(near[...], far[...], 1.0))
        return restore(*inv_refs, *value).astype(bf16)

    def corr_of(inv_refs, taps_spec, near, far):
        value = times_conj(window(near[...], far[...], -1.0), parts(taps_spec))
        return restore(*inv_refs, *value).astype(bf16)

    def by_side(q, left, right):
        pl.when(q < 2)(left)
        pl.when(q >= 2)(right)

    def inner(place_ref, high, low, inv_high, inv_low, p0, p1, g0, g1, *refs):
        keep, far_taps, spec, ship, filt, held = refs
        q = place_ref[0]
        chip = 2 * pad_taps
        for z in range(planes):
            at = slice(z * chip, (z + 1) * chip)
            filt[block_at(2 * z + q // 2, chip)] = keep[at]
            filt[block_at(2 * z + 1 - q // 2, chip)] = far_taps[at]
        taps_spec = spectrum(high, low, filt[...])
        spec[...] = taps_spec
        inv_refs = (inv_high, inv_low)

        def left():
            held[...] = mixed_of(inv_refs, spec[...], p1, p0)

        def right():
            held[...] = corr_of(inv_refs, spec[...], g0, g1)

        by_side(q, left, right)
        ship[:rows] = held[block_at(q % 2, rows)]
        ship[rows:] = held[block_at(1 - q % 2, rows)]

    def outer(place_ref, high, low, inv_high, inv_low, p0, g1, behind, halo, taps_ref, *refs):
        spec, ship, held = refs
        q = place_ref[0]
        ahead = spectrum(high, low, halo[...])
        spec[...] = ahead
        inv_refs = (inv_high, inv_low)

        def left():
            held[...] = corr_of(inv_refs, taps_ref[...], g1, spec)

        def right():
            held[...] = mixed_of(inv_refs, taps_ref[...], p0, behind)

        by_side(q, left, right)
        ship[:rows] = held[block_at(q % 2, rows)]
        ship[rows:] = held[block_at(1 - q % 2, rows)]

    def kept(place_ref, inv_high, inv_low, p0, p1, g0, g1, behind, ahead, taps_ref, *refs):
        mixed_own, corr_own, side, held = refs
        q = place_ref[0]
        inv_refs = (inv_high, inv_low)

        def run(p_near, p_far, g_near, g_far):
            held[...] = mixed_of(inv_refs, taps_ref[...], p_near, p_far)
            mixed_own[...] = held[block_at(q % 2, rows)]
            side[:rows] = held[block_at(1 - q % 2, rows)]
            held[...] = corr_of(inv_refs, taps_ref[...], g_near, g_far)
            corr_own[...] = held[block_at(q % 2, rows)]
            side[rows:] = held[block_at(1 - q % 2, rows)]

        by_side(q, lambda: run(p0, behind, g0, g1), lambda: run(p1, p0, g1, ahead))

    def pick(ref, index):
        if own_taps % 8 == 0:
            return ref[block_at(index, own_taps)]
        value = ref[:own_taps]
        for n in range(1, PLANE):
            value = jnp.where(index == n, ref[n * own_taps : (n + 1) * own_taps], value)
        return value

    def add_lags(place_ref, *refs):
        ins, (own, side, ship, full) = refs[:planes], refs[planes:]
        q = place_ref[0]
        total = ins[0][...]
        for ref in ins[1:]:
            total = total + ref[...].astype(f32)
        full[...] = total * (1.0 / math.sqrt(rows * nseq))
        own[...] = pick(full, q)
        side[...] = pick(full, q ^ 1)
        ship[:own_taps] = pick(full, q ^ 2)
        ship[own_taps:] = pick(full, q ^ 3)

    def join_first(side, far, out):
        out[: 2 * rows] = side[...]
        out[2 * rows :] = far[rows:]

    def join_second(far, lag_side, lag_far, out, lag_out):
        out[...] = far[rows:]
        lag_out[:own_taps] = lag_side[...]
        lag_out[own_taps:] = lag_far[own_taps:]

    def write(place_ref, steps, values, gates, outs, held, sems):
        copies = []
        for n, step in enumerate(steps):
            at = block_at(place_ref[0] ^ step, width)
            for m, (gate, out) in enumerate(zip(gates, outs)):
                value = values[n][min(m, 1)].astype(f32)
                held[m, n] = (value * gate[:, at].astype(f32)).astype(bf16)
                copy = pltpu.make_async_copy(held.at[m, n], out.at[:, at], sems.at[m, n])
                copy.start()
                copies.append(copy)
        return copies

    def finish_near(place_ref, mixed, corr, near, o_ref, v_ref, k_ref, *refs):
        outs, (mark, held, sems) = refs[:3], refs[3:]
        values = ((mixed[...], corr[...]), (near[:rows], near[rows : 2 * rows]))
        copies = write(place_ref, (0, 1), values, (o_ref, v_ref, k_ref), outs, held, sems)
        mark[...] = jnp.zeros_like(mark)
        for copy in copies:
            copy.wait()

    def finish_far(place_ref, first, second, near, last, o_ref, v_ref, k_ref, *refs):
        lag_own, lag_near, lag_far, dq, dk, dv, df, held, full, sems, sem = refs
        q = place_ref[0]
        left = q < 2
        values = []
        for one, two in ((first[:rows], second[:rows]), (near[2 * rows :], last[...])):
            values.append((jnp.where(left, two, one), jnp.where(left, one, two)))
        copies = write(place_ref, (2, 3), values, (o_ref, v_ref, k_ref), (dq, dk, dv), held, sems)
        full[:, block_at(q, width)] = lag_own[...]
        full[:, block_at(q ^ 1, width)] = lag_near[:own_taps]
        full[:, block_at(q ^ 2, width)] = lag_far[:own_taps]
        full[:, block_at(q ^ 3, width)] = lag_near[own_taps:]
        copy = pltpu.make_async_copy(full, df, sem)
        copy.start()
        for copy in copies + [copy]:
            copy.wait()

    block = struct(rows, width, bf16)
    double = struct(2 * rows, width, bf16)
    spectral = struct(2 * taps, width, f32)
    halo = struct(taps, width, bf16)

    def product_block(step):
        start = (me % PLANE ^ step) * width
        left = lax.dynamic_slice_in_dim(keys, start, width, 1).astype(f32)
        right = lax.dynamic_slice_in_dim(values, start, width, 1).astype(f32)
        return (left * right).astype(bf16)

    sent = [product_block(step) for step in range(PLANE)]
    far_p = [swap(sent[step], step) for step in (2, 3)]
    keep, side = call(
        gate_grad,
        flops=1,
        outs=[double, struct(3 * rows + 2 * pad_taps, width, bf16)],
        args=[None, out_grad, queries, sent[1], filter_taps],
        after=[],
    )
    near = swap(side, 1)

    product, top = call(
        gather_product,
        [struct(tokens, width, bf16), halo],
        [None, sent[0], near, *far_p],
        flops=1,
    )
    p_spec = own_spectra(product, 1, [])
    (packed,) = call(
        pack_taps,
        [struct(4 * pad_taps, width, bf16)],
        [None, filter_taps, near],
        after=[],
        flops=1,
    )
    far_taps = [swap(packed, PLANE * step) for step in range(1, planes)]
    far = swap(join(keep, near, after=[], flops=1000000000), 2)
    taps_keep, taps_ship = call(
        lay_taps,
        [struct(2 * column, width, bf16)] * 2,
        [None, packed, *far_taps],
        after=[p_spec[0]],
        flops=1000000000,
    )
    taps_far = swap(taps_ship, 2)

    behind = shift(top, PLANE)

    grad, bottom = call(
        gather_grad,
        [struct(tokens, width, bf16), halo],
        [None, keep, near, far],
        after=[],
        flops=1,
    )
    ahead = shift(bottom, -PLANE)
    g_spec = own_spectra(grad, 1, [])

    taps_spec, ship = call(
        inner,
        [spectral, double],
        [None, *fwd_lag, *inv, *p_spec, *g_spec, taps_keep, taps_far],
        scratch=[pltpu.VMEM((PLANE * column, width), bf16), pltpu.VMEM((taps, width), bf16)],
        after=[],
        flops=1,
    )
    first = swap(ship, 2)
    behind_spec, own_lags, *away = call(
        lags,
        [spectral, struct(plane_taps, width, f32)]
        + [struct(plane_taps, width, bf16)] * (planes - 1),
        [None, *fwd, *inv, *p_spec, *g_spec, behind],
        scratch=[pltpu.VMEM((taps, width), f32)],
        after=[taps_spec],
        flops=10000000000,
    )
    away = [swap(part, PLANE * (step + 1)) for step, part in enumerate(away)]
    ahead_spec, ship = call(
        outer,
        [spectral, double],
        [None, *fwd, *inv, p_spec[0], g_spec[1], behind_spec, ahead, taps_spec],
        scratch=[pltpu.VMEM((taps, width), bf16)],
        after=[taps_spec],
        flops=1,
    )
    second = swap(ship, 2)
    mixed_own, corr_own, side = call(
        kept,
        [block, block, double],
        [None, *inv, *p_spec, *g_spec, behind_spec, ahead_spec, taps_spec],
        scratch=[pltpu.VMEM((taps, width), bf16)],
        after=[first],
        flops=1,
    )
    triple = struct(3 * rows, width, bf16)
    (joined,) = call(
        join_first, [triple], [side, first], after=[], flops=1
    )
    near = swap(joined, 1)
    lag_double = struct(2 * own_taps, width, f32)
    lag_own, lag_side, lag_ship = call(
        add_lags,
        [struct(own_taps, width, f32)] * 2 + [lag_double],
        [None, own_lags, *away],
        scratch=[pltpu.VMEM((plane_taps, width), f32)],
        after=[corr_own],
        flops=10000000000,
    )
    lag_far = swap(lag_ship, 2)
    whole = struct(rows, channels, bf16)
    *partial, mark = call(
        finish_near,
        [whole] * 3 + [struct(8, 128, f32)],
        [None, mixed_own, corr_own, near, out_grad, values, keys],
        scratch=[
            pltpu.VMEM((3, 2, rows, width), bf16),
            pltpu.SemaphoreType.DMA((3, 2)),
        ],
        spaces=[pl.ANY] * 3 + [pltpu.VMEM],
        flops=1,
    )
    joined, lag_joined = call(
        join_second,
        [block, lag_double],
        [second, lag_side, lag_far],
        after=[mark],
        flops=1,
    )
    last = swap(joined, 1)
    lag_near = swap(lag_joined, 1)
    return call(
        finish_far,
        [whole] * 3 + [struct(own_taps, channels, f32)],
        [None, first, second, near, last, out_grad, values, keys, lag_own, lag_near, lag_far],
        scratch=[
            pltpu.VMEM((3, 2, rows, width), bf16),
            pltpu.VMEM((own_taps, channels), f32),
            pltpu.SemaphoreType.DMA((3, 2)),
            pltpu.SemaphoreType.DMA,
        ],
        spaces=[pl.ANY] * 4,
        aliases=partial,
    )


def solution(mesh):
    placed = (
        P(("grp", "seq"), None),
        P(("grp", "seq"), None),
        P(("grp", "seq"), None),
        P(("grp", "seq"), None),
        P("seq", None),
    )
    return jax.shard_map(
        shards,
        mesh=mesh,
        in_specs=placed,
        out_specs=(
            P(("grp", "seq"), None),
            P(("grp", "seq"), None),
            P(("grp", "seq"), None),
            P(("grp", "seq"), None),
        ),
        check_vma=False,
    )
```

```python
import math

import jax
import jax.numpy as jnp
import numpy as np
from jax import lax
from jax.experimental import pallas as pl
from jax.experimental.pallas import tpu as pltpu
from jax.sharding import PartitionSpec as P

PLANE = 4
VMEM_BYTES = 32 * 1024 * 1024


def tables(block):
    half = np.concatenate([np.arange(0, block, 2), np.arange(1, block, 2)])
    angle = np.pi * (half[:, None] + 0.5) * np.arange(block)[None, :] / block
    forward = np.concatenate([np.cos(angle), -np.sin(angle)], 0)
    inverse = forward.T / block
    return forward, inverse


def pair(table):
    high = table.astype(np.float32).astype(jnp.bfloat16)
    low = (table - high.astype(np.float64)).astype(np.float32).astype(jnp.bfloat16)
    return jnp.asarray(high), jnp.asarray(low)


def dot(left, right):
    return jnp.dot(left, right, preferred_element_type=jnp.float32)


def spectrum(high, low, block):
    return dot(high[...], block) + dot(low[...], block)


def restore(high, low, real, imag):
    spec = jnp.concatenate([real, imag], 0)
    top = spec.astype(jnp.bfloat16)
    return dot(high[...], top) + dot(low[...], top)


def parts(spec):
    half = spec.shape[0] // 2
    return spec[:half], spec[half:]


def turned(spec, sign):
    real, imag = parts(spec)
    quarter = real.shape[0] // 2
    flip = lambda a, s: jnp.concatenate([s * a[:quarter], -s * a[quarter:]], 0)
    return flip(imag, -sign), flip(real, sign)


def window(near, far, sign):
    real, imag = parts(near)
    other_real, other_imag = turned(far, sign)
    return real + other_real, imag + other_imag


def times(left, right):
    return left[0] * right[0] - left[1] * right[1], left[0] * right[1] + left[1] * right[0]


def times_conj(left, right):
    return left[0] * right[0] + left[1] * right[1], left[1] * right[0] - left[0] * right[1]


class Here:
    def __getitem__(self, index):
        me = lax.axis_index("seq")
        return me // PLANE if index else me % PLANE


def call(body, outs, args, scratch=(), spaces=None, after=(), flops=1, aliases=()):
    located = args[0] is None
    args = args[1:] if located else args
    specs = [
        pl.BlockSpec(memory_space=pltpu.VMEM) for _ in args
    ]
    after = [*after, *aliases]
    specs += [pl.BlockSpec(memory_space=pl.ANY)] * len(after)
    base = len(args) + len(after) - len(aliases)

    def run(*refs):
        first = [Here()] if located else []
        body(*first, *refs[: len(args)], *refs[len(args) + len(after) :])

    spaces = spaces or [pltpu.VMEM] * len(outs)
    return pl.pallas_call(
        run,
        out_shape=outs,
        in_specs=specs,
        out_specs=[pl.BlockSpec(memory_space=space) for space in spaces],
        scratch_shapes=scratch,
        input_output_aliases={base + n: n for n in range(len(aliases))},
        compiler_params=pltpu.CompilerParams(vmem_limit_bytes=VMEM_BYTES),
        cost_estimate=pl.CostEstimate(flops=flops, bytes_accessed=1, transcendentals=0),
    )(*args, *after)


def shards(queries, keys, values, out_grad, filter_taps):
    f32, bf16 = jnp.float32, jnp.bfloat16
    rows, channels = queries.shape
    nseq = lax.axis_size("seq")
    own_taps = filter_taps.shape[0]
    taps = own_taps * nseq
    planes = nseq // PLANE
    width = channels // PLANE
    tokens = rows * PLANE
    pad_taps = max(16, own_taps)
    plane_taps = taps // planes
    column = planes * pad_taps
    assert tokens == 2 * taps
    me = lax.axis_index("seq")
    devices = range(nseq)

    forward, inverse = tables(taps)
    fwd = pair(forward)
    inv = pair(inverse)
    lag_of = np.full((planes * PLANE, pad_taps), -1)
    lag_of[:, :own_taps] = np.arange(taps).reshape(planes * PLANE, own_taps)
    lag_of = lag_of.reshape(-1)
    if pad_taps == own_taps:
        fwd_lag = fwd
    else:
        fwd_lag = pair(np.where(lag_of[None, :] >= 0, forward[:, np.maximum(lag_of, 0)], 0.0))

    def swap(array, distance):
        return lax.ppermute(array, "seq", [(i, i ^ distance) for i in devices])

    def shift(array, distance):
        return lax.ppermute(
            array, "seq", [(i, i + distance) for i in devices if i + distance in devices]
        )

    def struct(r, c, dtype):
        return jax.ShapeDtypeStruct((r, c), dtype)

    def block_at(index, size):
        return pl.ds(pl.multiple_of(index * size, size), size)

    def lay_taps(place_ref, *refs):
        ins, (keep, ship) = refs[:planes], refs[planes:]
        q, z = place_ref[0], place_ref[1]
        for step in range(planes):
            for core in range(2):
                at = block_at(2 * (z ^ step) + (q % 2 ^ core), pad_taps)
                first = 2 * core * pad_taps
                keep[at] = ins[step][first : first + pad_taps]
                ship[at] = ins[step][first + pad_taps : first + 2 * pad_taps]

    def taps_block(taps_ref, at):
        block = taps_ref[:, at]
        if pad_taps > own_taps:
            fill = jnp.zeros((pad_taps - own_taps, width), f32)
            block = jnp.concatenate([block, fill], 0)
        return block.astype(bf16)

    def pack_taps(place_ref, taps_ref, near_ref, out):
        q = place_ref[0]
        out[:pad_taps] = taps_block(taps_ref, block_at(q, width))
        out[pad_taps : 2 * pad_taps] = taps_block(taps_ref, block_at(q ^ 2, width))
        out[2 * pad_taps :] = near_ref[3 * rows :]

    def gate_grad(place_ref, o_ref, q_ref, p_ref, taps_ref, keep, side):
        q = place_ref[0]
        side[:rows] = p_ref[...]
        for step, (out, first) in enumerate(((keep, 0), (side, rows), (keep, rows), (side, 2 * rows))):
            at = block_at(q ^ step, width)
            out[first : first + rows] = (
                o_ref[:, at].astype(f32) * q_ref[:, at].astype(f32)
            ).astype(bf16)
        for n, step in enumerate((1, 3)):
            first = 3 * rows + n * pad_taps
            side[first : first + pad_taps] = taps_block(taps_ref, block_at(q ^ step, width))

    def join(left, right, after=(), flops=1):
        def body(left_ref, right_ref, out):
            out[:rows] = left_ref[rows : 2 * rows]
            out[rows:] = right_ref[2 * rows : 3 * rows]

        return call(body, [struct(2 * rows, width, bf16)], [left, right], after=after, flops=flops)[0]

    def gather_product(place_ref, *refs):
        ins, (product, top) = refs[:PLANE], refs[PLANE:]
        q = place_ref[0]
        for step in range(PLANE):
            product[block_at(q ^ step, rows)] = ins[step][:rows]
        top[...] = product[tokens - taps :]

    def gather_grad(place_ref, keep, near, far, grad, bottom):
        q = place_ref[0]
        grad[block_at(q, rows)] = keep[:rows]
        grad[block_at(q ^ 1, rows)] = near[rows : 2 * rows]
        grad[block_at(q ^ 2, rows)] = far[:rows]
        grad[block_at(q ^ 3, rows)] = far[rows:]
        bottom[...] = grad[:taps]

    def own_spectra(array, flops, after):
        def body(high, low, ref, *outs):
            for block in range(2):
                outs[block][...] = spectrum(high, low, ref[block * taps : (block + 1) * taps])

        return call(body, [struct(2 * taps, width, f32)] * 2, [*fwd, array], flops=flops, after=after)

    def lags(place_ref, high, low, inv_high, inv_low, p0, p1, g0, g1, halo, *refs):
        spec, outs, full = refs[0], refs[1:-1], refs[-1]
        behind = spectrum(high, low, halo[...])
        spec[...] = behind
        one = times_conj(parts(g0[...]), window(p0[...], behind, 1.0))
        two = times_conj(parts(g1[...]), window(p1[...], p0[...], 1.0))
        full[...] = restore(inv_high, inv_low, one[0] + two[0], one[1] + two[1])
        for step in range(planes):
            block = full[block_at(place_ref[1] ^ step, plane_taps)]
            outs[step][...] = block.astype(outs[step].dtype)

    def mixed_of(inv_refs, taps_spec, near, far):
        value = times(parts(taps_spec), window(near[...], far[...], 1.0))
        return restore(*inv_refs, *value).astype(bf16)

    def corr_of(inv_refs, taps_spec, near, far):
        value = times_conj(window(near[...], far[...], -1.0), parts(taps_spec))
        return restore(*inv_refs, *value).astype(bf16)

    def by_side(q, left, right):
        pl.when(q < 2)(left)
        pl.when(q >= 2)(right)

    def inner(place_ref, high, low, inv_high, inv_low, p0, p1, g0, g1, *refs):
        keep, far_taps, spec, ship, filt, held = refs
        q = place_ref[0]
        chip = 2 * pad_taps
        for z in range(planes):
            at = slice(z * chip, (z + 1) * chip)
            filt[block_at(2 * z + q // 2, chip)] = keep[at]
            filt[block_at(2 * z + 1 - q // 2, chip)] = far_taps[at]
        taps_spec = spectrum(high, low, filt[...])
        spec[...] = taps_spec
        inv_refs = (inv_high, inv_low)

        def left():
            held[...] = mixed_of(inv_refs, spec[...], p1, p0)

        def right():
            held[...] = corr_of(inv_refs, spec[...], g0, g1)

        by_side(q, left, right)
        ship[:rows] = held[block_at(q % 2, rows)]
        ship[rows:] = held[block_at(1 - q % 2, rows)]

    def outer(place_ref, high, low, inv_high, inv_low, p0, g1, behind, halo, taps_ref, *refs):
        spec, ship, held = refs
        q = place_ref[0]
        ahead = spectrum(high, low, halo[...])
        spec[...] = ahead
        inv_refs = (inv_high, inv_low)

        def left():
            held[...] = corr_of(inv_refs, taps_ref[...], g1, spec)

        def right():
            held[...] = mixed_of(inv_refs, taps_ref[...], p0, behind)

        by_side(q, left, right)
        ship[:rows] = held[block_at(q % 2, rows)]
        ship[rows:] = held[block_at(1 - q % 2, rows)]

    def kept(place_ref, inv_high, inv_low, p0, p1, g0, g1, behind, ahead, taps_ref, *refs):
        mixed_own, corr_own, side, held = refs
        q = place_ref[0]
        inv_refs = (inv_high, inv_low)

        def run(p_near, p_far, g_near, g_far):
            held[...] = mixed_of(inv_refs, taps_ref[...], p_near, p_far)
            mixed_own[...] = held[block_at(q % 2, rows)]
            side[:rows] = held[block_at(1 - q % 2, rows)]
            held[...] = corr_of(inv_refs, taps_ref[...], g_near, g_far)
            corr_own[...] = held[block_at(q % 2, rows)]
            side[rows:] = held[block_at(1 - q % 2, rows)]

        by_side(q, lambda: run(p0, behind, g0, g1), lambda: run(p1, p0, g1, ahead))

    def pick(ref, index):
        if own_taps % 8 == 0:
            return ref[block_at(index, own_taps)]
        value = ref[:own_taps]
        for n in range(1, PLANE):
            value = jnp.where(index == n, ref[n * own_taps : (n + 1) * own_taps], value)
        return value

    def add_lags(place_ref, *refs):
        ins, (own, side, ship, full) = refs[:planes], refs[planes:]
        q = place_ref[0]
        total = ins[0][...]
        for ref in ins[1:]:
            total = total + ref[...].astype(f32)
        full[...] = total * (1.0 / math.sqrt(rows * nseq))
        own[...] = pick(full, q)
        side[...] = pick(full, q ^ 1)
        ship[:own_taps] = pick(full, q ^ 2)
        ship[own_taps:] = pick(full, q ^ 3)

    def join_first(side, far, out):
        out[: 2 * rows] = side[...]
        out[2 * rows :] = far[rows:]

    def join_second(far, lag_side, lag_far, out, lag_out):
        out[...] = far[rows:]
        lag_out[:own_taps] = lag_side[...]
        lag_out[own_taps:] = lag_far[own_taps:]

    def write(place_ref, steps, values, gates, outs, held, sems):
        copies = []
        for n, step in enumerate(steps):
            at = block_at(place_ref[0] ^ step, width)
            for m, (gate, out) in enumerate(zip(gates, outs)):
                value = values[n][min(m, 1)].astype(f32)
                held[m, n] = (value * gate[:, at].astype(f32)).astype(bf16)
                copy = pltpu.make_async_copy(held.at[m, n], out.at[:, at], sems.at[m, n])
                copy.start()
                copies.append(copy)
        return copies

    def finish_near(place_ref, mixed, corr, near, o_ref, v_ref, k_ref, *refs):
        outs, (mark, held, sems) = refs[:3], refs[3:]
        values = ((mixed[...], corr[...]), (near[:rows], near[rows : 2 * rows]))
        copies = write(place_ref, (0, 1), values, (o_ref, v_ref, k_ref), outs, held, sems)
        mark[...] = jnp.zeros_like(mark)
        for copy in copies:
            copy.wait()

    def finish_far(place_ref, first, second, near, last, o_ref, v_ref, k_ref, *refs):
        lag_own, lag_near, lag_far, dq, dk, dv, df, held, full, sems, sem = refs
        q = place_ref[0]
        left = q < 2
        values = []
        for one, two in ((first[:rows], second[:rows]), (near[2 * rows :], last[...])):
            values.append((jnp.where(left, two, one), jnp.where(left, one, two)))
        copies = write(place_ref, (2, 3), values, (o_ref, v_ref, k_ref), (dq, dk, dv), held, sems)
        full[:, block_at(q, width)] = lag_own[...]
        full[:, block_at(q ^ 1, width)] = lag_near[:own_taps]
        full[:, block_at(q ^ 2, width)] = lag_far[:own_taps]
        full[:, block_at(q ^ 3, width)] = lag_near[own_taps:]
        copy = pltpu.make_async_copy(full, df, sem)
        copy.start()
        for copy in copies + [copy]:
            copy.wait()

    block = struct(rows, width, bf16)
    double = struct(2 * rows, width, bf16)
    spectral = struct(2 * taps, width, f32)
    halo = struct(taps, width, bf16)

    def product_block(step):
        start = (me % PLANE ^ step) * width
        left = lax.dynamic_slice_in_dim(keys, start, width, 1).astype(f32)
        right = lax.dynamic_slice_in_dim(values, start, width, 1).astype(f32)
        return (left * right).astype(bf16)

    sent = [product_block(step) for step in (2, 3)]
    sent = [product_block(0), product_block(1)] + list(lax.optimization_barrier(tuple(sent)))
    far_p = [swap(sent[step], step) for step in (2, 3)]
    keep, side = call(
        gate_grad,
        flops=1,
        outs=[double, struct(3 * rows + 2 * pad_taps, width, bf16)],
        args=[None, out_grad, queries, sent[1], filter_taps],
        after=[],
    )
    near = swap(side, 1)

    product, top = call(
        gather_product,
        [struct(tokens, width, bf16), halo],
        [None, sent[0], near, *far_p],
        flops=1,
    )
    p_spec = own_spectra(product, 1, [])
    (packed,) = call(
        pack_taps,
        [struct(4 * pad_taps, width, bf16)],
        [None, filter_taps, near],
        after=[],
        flops=1,
    )
    far_taps = [swap(packed, PLANE * step) for step in range(1, planes)]
    far = swap(join(keep, near, after=[], flops=1000000000), 2)
    taps_keep, taps_ship = call(
        lay_taps,
        [struct(2 * column, width, bf16)] * 2,
        [None, packed, *far_taps],
        after=[p_spec[0]],
        flops=1000000000,
    )
    taps_far = swap(taps_ship, 2)

    behind = shift(top, PLANE)

    grad, bottom = call(
        gather_grad,
        [struct(tokens, width, bf16), halo],
        [None, keep, near, far],
        after=[],
        flops=1,
    )
    ahead = shift(bottom, -PLANE)
    g_spec = own_spectra(grad, 1, [])

    taps_spec, ship = call(
        inner,
        [spectral, double],
        [None, *fwd_lag, *inv, *p_spec, *g_spec, taps_keep, taps_far],
        scratch=[pltpu.VMEM((PLANE * column, width), bf16), pltpu.VMEM((taps, width), bf16)],
        after=[],
        flops=1,
    )
    first = swap(ship, 2)
    behind_spec, own_lags, *away = call(
        lags,
        [spectral, struct(plane_taps, width, f32)]
        + [struct(plane_taps, width, bf16)] * (planes - 1),
        [None, *fwd, *inv, *p_spec, *g_spec, behind],
        scratch=[pltpu.VMEM((taps, width), f32)],
        after=[taps_spec],
        flops=10000000000,
    )
    away = [swap(part, PLANE * (step + 1)) for step, part in enumerate(away)]
    ahead_spec, ship = call(
        outer,
        [spectral, double],
        [None, *fwd, *inv, p_spec[0], g_spec[1], behind_spec, ahead, taps_spec],
        scratch=[pltpu.VMEM((taps, width), bf16)],
        after=[taps_spec],
        flops=1,
    )
    second = swap(ship, 2)
    mixed_own, corr_own, side = call(
        kept,
        [block, block, double],
        [None, *inv, *p_spec, *g_spec, behind_spec, ahead_spec, taps_spec],
        scratch=[pltpu.VMEM((taps, width), bf16)],
        after=[first],
        flops=1,
    )
    triple = struct(3 * rows, width, bf16)
    (joined,) = call(
        join_first, [triple], [side, first], after=[], flops=1
    )
    near = swap(joined, 1)
    lag_double = struct(2 * own_taps, width, f32)
    lag_own, lag_side, lag_ship = call(
        add_lags,
        [struct(own_taps, width, f32)] * 2 + [lag_double],
        [None, own_lags, *away],
        scratch=[pltpu.VMEM((plane_taps, width), f32)],
        after=[corr_own],
        flops=10000000000,
    )
    lag_far = swap(lag_ship, 2)
    whole = struct(rows, channels, bf16)
    *partial, mark = call(
        finish_near,
        [whole] * 3 + [struct(8, 128, f32)],
        [None, mixed_own, corr_own, near, out_grad, values, keys],
        scratch=[
            pltpu.VMEM((3, 2, rows, width), bf16),
            pltpu.SemaphoreType.DMA((3, 2)),
        ],
        spaces=[pl.ANY] * 3 + [pltpu.VMEM],
        flops=1,
    )
    joined, lag_joined = call(
        join_second,
        [block, lag_double],
        [second, lag_side, lag_far],
        after=[mark],
        flops=1,
    )
    last = swap(joined, 1)
    lag_near = swap(lag_joined, 1)
    return call(
        finish_far,
        [whole] * 3 + [struct(own_taps, channels, f32)],
        [None, first, second, near, last, out_grad, values, keys, lag_own, lag_near, lag_far],
        scratch=[
            pltpu.VMEM((3, 2, rows, width), bf16),
            pltpu.VMEM((own_taps, channels), f32),
            pltpu.SemaphoreType.DMA((3, 2)),
            pltpu.SemaphoreType.DMA,
        ],
        spaces=[pl.ANY] * 4,
        aliases=partial,
    )


def solution(mesh):
    placed = (
        P(("grp", "seq"), None),
        P(("grp", "seq"), None),
        P(("grp", "seq"), None),
        P(("grp", "seq"), None),
        P("seq", None),
    )
    return jax.shard_map(
        shards,
        mesh=mesh,
        in_specs=placed,
        out_specs=(
            P(("grp", "seq"), None),
            P(("grp", "seq"), None),
            P(("grp", "seq"), None),
            P(("grp", "seq"), None),
        ),
        check_vma=False,
    )
```
